256 devices in a mesh: dp: 64 (over x_hi, y, z), mp: 4 (over x_lo, core).
Axes of the slice: x: 4 (x_hi: 2, x_lo: 2; x = x_hi * 2 + x_lo), y: 4, z: 8, core: 2. Of those that a mesh axis runs over, the one named last changes fastest.
Arguments:
- head_out: bfloat16 [3, 8192, 4096], P(None, 'dp', 'mp'), may hold values from -6 to 6
- residual: bfloat16 [3, 8192, 4096], P(None, 'dp', 'mp'), may hold values from -6 to 6
- out_weight: bfloat16 [4096, 4096], P('dp', 'mp'), may hold values from -0.09375 to 0.09375
- strategy_table: bfloat16 [64, 4096], P(None, 'mp'), may hold values from -3 to 3
- meta_graph: int32 [64, 64], replicated, may hold values from 0 to 3, as said below
- strategy_ids: int32 [3, 8192], P(None, 'dp'), may hold values from 0 to 63
- cotangent: bfloat16 [3, 8192, 4096], P(None, 'dp', 'mp'), may hold values from -16 to 16
Outputs:
- layer_out: bfloat16 [3, 8192, 4096], P(None, 'dp', 'mp')
- head_grad: bfloat16 [3, 8192, 4096], P(None, 'dp', 'mp')
- weight_grad: float32 [4096, 4096], P('dp', 'mp')
- table_grad: float32 [64, 4096], P(None, 'mp')
The draws below stay inside these ranges and needn't reach their ends.
Inputs may be any that keep to these rules, and one draw needn't show every extreme that they name: `meta_graph`: entries are zero on and above the diagonal; the last strategy meets the first with weight 3.
All inputs are finite; a program needn't handle non-finite values.
Results may differ from the reference program's by a relative error of at most 0.009.
Values may be sent and summed in bfloat16 or wider, within the bound.
No kernel may reach another device: no remote copies, remote signals or barrier semaphores. Data moves between devices by JAX's collectives and lax.ppermute only.
A program may use at most 128 MiB of HBM per device.

```python
import jax
import jax.numpy as jnp
from jax import lax

D = 4096
HEADS = 32
HD = 128
STRATS = 64
MB = 3
TOKENS = 8192
N_MP = 4


def draw_meta_graph(key, part):
    values = jax.random.randint(key, (STRATS, STRATS), 0, 4, dtype=jnp.int32)
    rows = lax.broadcasted_iota(jnp.int32, (STRATS, STRATS), 0)
    cols = lax.broadcasted_iota(jnp.int32, (STRATS, STRATS), 1)
    values = jnp.where(cols < rows, values, 0)
    values = jnp.where((rows == STRATS - 1) & (cols == 0), 3, values)
    return values.astype(jnp.int32)


def set_ends(result, stream_key, low, top_value):
    extent = result.shape
    spot = [jax.random.randint(jax.random.fold_in(stream_key, axis), (), 0, extent[axis]) for axis in range(len(extent))]
    result = result.at[tuple(spot)].set(low)
    longest = extent.index(max(extent))
    spot[longest] = (spot[longest] + 1) % extent[longest]
    return result.at[tuple(spot)].set(top_value)


def with_spikes(array, rng, source, target, shards_of, factor):
    def block_of(position):
        return (jnp.arange(array.shape[position]) // (array.shape[position] // shards_of)).reshape((-1,) + (1,) * (array.ndim - 1 - position))

    one_side = jax.random.permutation(rng, shards_of)[block_of(target)]
    other_side = (block_of(target) + shards_of // 2) % shards_of
    return jnp.where((block_of(source) == one_side) | (block_of(source) == other_side), factor * array, array)


def levels(stream_key, extent, pieces, low, top_value):
    level = 1.0
    for dim, parts in pieces:
        draws = jax.random.uniform(jax.random.fold_in(jax.random.fold_in(stream_key, 6), dim), (parts,), jnp.float32, low / len(pieces), top_value / len(pieces))
        level = level * jnp.repeat(jnp.exp(draws), extent[dim] // parts).reshape((-1,) + (1,) * (len(extent) - 1 - dim))
    return level


def centred(stream_key, extent, spread, limit, pieces=(), kind=jnp.bfloat16):
    array = spread * jax.random.normal(stream_key, extent, jnp.float32)
    if pieces:
        array = array * levels(stream_key, extent, pieces, -0.22, 0.18)
    return jnp.clip(array, -limit, limit).astype(kind)


def gaussian_with(key, dims, deviation, reach, cuts, heavy, kind=jnp.bfloat16):
    array = deviation * jax.random.normal(key, dims, jnp.float32)
    if cuts:
        array = array * levels(key, dims, cuts, -0.22, 0.18)
    return jnp.clip(with_spikes(array, jax.random.fold_in(key, 3), *heavy), -reach, reach).astype(kind)


def setup_inputs(seed: int = 0) -> dict:
    streams_of = jax.random.split(jax.random.key(seed), 8)
    head_out = centred(streams_of[0], (MB, TOKENS, HEADS * HD), 1.0, 6.0, ((1, 64), (2, 4)))
    residual = centred(streams_of[1], (MB, TOKENS, D), 1.0, 6.0, ((1, 64), (2, 4)))
    out_weight = centred(streams_of[2], (D, HEADS * HD), (HEADS * HD) ** -0.5, 0.09375, ((0, 64), (1, 4)))
    strategy_table = centred(streams_of[3], (STRATS, D), 0.5, 3.0, ((1, 4),))
    meta_graph = draw_meta_graph(jax.random.fold_in(streams_of[7], 71), 0)
    strategy_ids = set_ends(jax.random.randint(streams_of[5], (MB, TOKENS), 0, STRATS), jax.random.fold_in(streams_of[5], 1), 0, STRATS - 1).astype(jnp.int32)
    cotangent = gaussian_with(streams_of[6], (MB, TOKENS, D), 1.0, 16.0, ((1, 64), (2, 4)), (1, 2, 64, 4.0))
    return dict(head_out=head_out, residual=residual, out_weight=out_weight, strategy_table=strategy_table, meta_graph=meta_graph, strategy_ids=strategy_ids, cotangent=cotangent)


def mixture(meta_graph):
    counts = meta_graph.astype(jnp.float32)
    totals = jnp.maximum(lax.optimization_barrier(jnp.sum(counts, axis=1, keepdims=True)), 1.0)
    return jnp.eye(STRATS, dtype=jnp.float32) + counts / totals

def reference(head_out, residual, out_weight, strategy_table, meta_graph, strategy_ids, cotangent):
    highest = lax.Precision.HIGHEST
    mixing = mixture(meta_graph)
    table = jnp.dot(mixing, strategy_table.astype(jnp.float32), precision=highest)
    group_cols = HEADS * HD // N_MP
    grad_scale = 1.0 / jnp.sqrt(jnp.float32(MB * TOKENS))
    weight_sum = jnp.zeros((D, HEADS * HD), jnp.float32)
    table_sum = jnp.zeros((STRATS, D), jnp.float32)
    outputs = []
    head_grads = []
    for batch in range(MB):
        current = head_out[batch]
        projected = jnp.zeros((TOKENS, D), jnp.float32)
        for group in range(N_MP):
            lower = group * group_cols
            partial_sum = lax.dot_general(current[:, lower:lower + group_cols], out_weight[:, lower:lower + group_cols], (((1,), (1,)), ((), ())), preferred_element_type=jnp.float32)
            rounded = lax.optimization_barrier(partial_sum.astype(jnp.bfloat16))
            projected = projected + rounded.astype(jnp.float32)
        one_hot = (strategy_ids[batch][:, None] == jnp.arange(STRATS, dtype=jnp.int32)[None, :]).astype(jnp.float32)
        gating = 1.0 + jnp.dot(one_hot, table, precision=highest)
        outputs.append((residual[batch].astype(jnp.float32) + projected * gating).astype(jnp.bfloat16))
        grad_rows = (cotangent[batch].astype(jnp.float32) * gating).astype(jnp.bfloat16)
        head_grads.append(jnp.dot(grad_rows, out_weight, preferred_element_type=jnp.float32).astype(jnp.bfloat16))
        weight_sum = weight_sum + lax.dot_general(grad_rows, current, (((0,), (0,)), ((), ())), preferred_element_type=jnp.float32)
        cond_grad = cotangent[batch].astype(jnp.float32) * projected
        table_sum = table_sum + lax.dot_general(one_hot, cond_grad, (((0,), (0,)), ((), ())), precision=highest, preferred_element_type=jnp.float32)
    weight_grad = weight_sum * grad_scale
    table_grad = jnp.dot(mixing.T, table_sum, precision=highest) * grad_scale
    return (jnp.stack(outputs), jnp.stack(head_grads), weight_grad, table_grad)
```

```python
import math

import jax
import jax.numpy as jnp
from jax import lax
from jax.sharding import Mesh, PartitionSpec as P

XH, NY, NZ, XL, NC = 2, 4, 8, 2, 2
BF = jnp.bfloat16
F32 = jnp.float32


def shift(a, axis, n, k):
    return lax.ppermute(a, axis, [(i, (i + k) % n) for i in range(n)])


def mixture(meta_graph):
    counts = meta_graph.astype(F32)
    totals = jnp.maximum(jnp.sum(counts, axis=1, keepdims=True), 1.0)
    return jnp.eye(meta_graph.shape[0], dtype=F32) + counts / totals


def ring_gather(a, axis, n):
    got = {0: a}
    up = down = a
    for k in range(1, n // 2):
        up = shift(up, axis, n, 1)
        down = shift(down, axis, n, -1)
        got[k], got[n - k] = up, down
    half = a.shape[-1] // 2 // 128 * 128
    left = shift(up[..., :half], axis, n, 1)
    right = shift(down[..., half:], axis, n, -1)
    got[n // 2] = jnp.concatenate([left, right], axis=-1)
    return got


def ring_scatter(block, axis, n):
    add = lambda recv, k, *s: (recv.astype(F32) + block(k)[s].astype(F32))
    far = block(n // 2)
    half = far.shape[-1] // 2 // 128 * 128
    up, down = far[..., :half], far[..., half:]
    up = shift(up.astype(BF), axis, n, 1)
    down = shift(down.astype(BF), axis, n, -1)
    for k in range(n // 2 - 1, 0, -1):
        mine_up, mine_down = block(k).astype(F32), block(n - k).astype(F32)
        if k == n // 2 - 1:
            up = jnp.concatenate([up.astype(F32) + mine_up[..., :half], mine_up[..., half:]], axis=-1)
            down = jnp.concatenate([mine_down[..., :half], down.astype(F32) + mine_down[..., half:]], axis=-1)
        else:
            up = up.astype(F32) + mine_up
            down = down.astype(F32) + mine_down
        up = shift(up.astype(BF), axis, n, 1)
        down = shift(down.astype(BF), axis, n, -1)
    return block(0).astype(F32) + up.astype(F32) + down.astype(F32)


def place(got, at, n, dim):
    first = got[0]
    out = jnp.zeros(first.shape[:dim] + (n,) + first.shape[dim:], first.dtype)
    for k, piece in got.items():
        out = lax.dynamic_update_index_in_dim(out, piece, (at - k) % n, dim)
    return out


def sum_table(t):
    z, y = lax.axis_index("z"), lax.axis_index("y")
    cols = t.shape[1]
    part = t.reshape(NZ, -1, cols)
    pick = lambda k: lax.dynamic_index_in_dim(part, (z + k) % NZ, 0, keepdims=False)
    acc = pick(0)
    for k in range(1, NZ):
        acc = acc + shift(pick(k), "z", NZ, k)
    width = cols // NY
    pick_y = lambda k: lax.dynamic_slice_in_dim(acc, ((y + k) % NY) * width, width, 1)
    tot = pick_y(0)
    for k in range(1, NY):
        tot = tot + shift(pick_y(k), "y", NY, k)
    tot = tot + shift(tot, "xh", XH, 1)
    row = jnp.zeros((NY,) + tot.shape, F32)
    for k in range(NY):
        row = lax.dynamic_update_index_in_dim(row, shift(tot, "y", NY, k) if k else tot, (y - k) % NY, 0)
    row = row.transpose(1, 0, 2).reshape(-1, cols)
    full = jnp.zeros(part.shape, F32)
    for k in range(NZ):
        full = lax.dynamic_update_index_in_dim(full, shift(row, "z", NZ, k) if k else row, (z - k) % NZ, 0)
    return full.reshape(t.shape)


def on_device(head_out, residual, out_weight, strategy_table, meta_graph, strategy_ids, cotangent):
    highest = lax.Precision.HIGHEST
    batches, local_rows, cols = head_out.shape
    rows = batches * local_rows
    strategies = meta_graph.shape[0]
    wr = out_weight.shape[0]
    cut = 640
    xh, y, z = lax.axis_index("xh"), lax.axis_index("y"), lax.axis_index("z")
    xl, c = lax.axis_index("xl"), lax.axis_index("c")
    grad_scale = 1.0 / math.sqrt(rows * XH * NY * NZ)

    ho = head_out.reshape(rows, cols)
    cot = cotangent.reshape(rows, cols).astype(F32)

    other = shift(out_weight, "xh", XH, 1)
    unit = jnp.stack([jnp.where(xh == 0, out_weight, other), jnp.where(xh == 0, other, out_weight)])
    unit_a, unit_b = unit[..., :cut], unit[..., cut:]
    za = place(ring_gather(unit_a, "z", NZ), z, NZ, 1)
    yb = place(ring_gather(unit_b, "y", NY), y, NY, 1)
    weight_a = place(ring_gather(za, "y", NY), y, NY, 1).reshape(-1, cut)
    weight_b = place(ring_gather(yb, "z", NZ), z, NZ, 2).reshape(-1, cols - cut)

    mixing = mixture(meta_graph)
    table = jnp.dot(mixing, strategy_table.astype(F32), precision=highest)
    one_hot = (
        strategy_ids.reshape(rows)[:, None] == lax.broadcasted_iota(jnp.int32, (1, strategies), 1)
    ).astype(F32)
    gating = 1.0 + jnp.dot(one_hot, table, precision=highest)
    grad_t = (cot * gating).astype(BF).T

    far = shift(grad_t, "xl", XL, 1)
    near = shift(grad_t, "c", NC, 1)
    far_near = shift(far, "c", NC, 1)
    full_t = jnp.zeros((XL * NC,) + grad_t.shape, BF)
    for piece, dx, dc in ((grad_t, 0, 0), (near, 0, 1), (far, 1, 0), (far_near, 1, 1)):
        full_t = lax.dynamic_update_index_in_dim(full_t, piece, (xl ^ dx) * 2 + (c ^ dc), 0)
    full_t = full_t.reshape(XH, NY, NZ, wr, rows)

    def block_a(k):
        g = lax.dynamic_index_in_dim(full_t, (y + k) % NY, 1, keepdims=False)
        return jnp.dot(g.reshape(-1, rows), ho[:, :cut], preferred_element_type=F32).reshape(XH, NZ, wr, cut)

    def block_b(k):
        g = lax.dynamic_index_in_dim(full_t, (z + k) % NZ, 2, keepdims=False)
        return jnp.dot(g.reshape(-1, rows), ho[:, cut:], preferred_element_type=F32).reshape(XH, NY, wr, cols - cut)

    ga = ring_scatter(block_a, "y", NY)
    ga = ring_scatter(lambda k: lax.dynamic_index_in_dim(ga, (z + k) % NZ, 1, keepdims=False), "z", NZ)
    gb = ring_scatter(block_b, "z", NZ)
    gb = ring_scatter(lambda k: lax.dynamic_index_in_dim(gb, (y + k) % NY, 1, keepdims=False), "y", NY)
    g = jnp.concatenate([ga, gb], axis=-1)
    mine = lax.dynamic_index_in_dim(g, xh, 0, keepdims=False)
    give = lax.dynamic_index_in_dim(g, 1 - xh, 0, keepdims=False)
    weight_sum = mine + shift(give.astype(BF), "xh", XH, 1).astype(F32)

    partial_sum = lax.dot_general(
        ho[:, :cut], weight_a, (((1,), (1,)), ((), ())), preferred_element_type=F32
    ) + lax.dot_general(ho[:, cut:], weight_b, (((1,), (1,)), ((), ())), preferred_element_type=F32)
    parts = partial_sum.astype(BF).reshape(rows, XL, NC, cols)
    keep = lax.dynamic_index_in_dim(parts, c, 2, keepdims=False)
    send = lax.dynamic_index_in_dim(parts, 1 - c, 2, keepdims=False)
    chip = keep.astype(F32) + shift(send, "c", NC, 1).astype(F32)
    proj = lax.dynamic_index_in_dim(chip, xl, 1, keepdims=False)
    away = lax.dynamic_index_in_dim(chip, 1 - xl, 1, keepdims=False).astype(BF)
    projected = proj + shift(away, "xl", XL, 1).astype(F32)

    layer_out = (residual.reshape(rows, cols).astype(F32) + projected * gating).astype(BF)
    table_part = lax.dot_general(
        one_hot, cot * projected, (((0,), (0,)), ((), ())), precision=highest, preferred_element_type=F32
    )
    table_grad = jnp.dot(mixing.T, sum_table(table_part), precision=highest) * grad_scale

    flat_t = full_t.reshape(-1, rows)
    over_d = (((0,), (0,)), ((), ()))
    head_grad = jnp.concatenate(
        [
            lax.dot_general(flat_t, w, over_d, preferred_element_type=F32).astype(BF)
            for w in (weight_a, weight_b)
        ],
        axis=1,
    )
    shape = head_out.shape
    return layer_out.reshape(shape), head_grad.reshape(shape), weight_sum * grad_scale, table_grad


def solution(mesh):
    fine = Mesh(mesh.devices.reshape(XH, NY, NZ, XL, NC), ("xh", "y", "z", "xl", "c"))
    dp, mp = ("xh", "y", "z"), ("xl", "c")
    tokens = P(None, dp, mp)
    return jax.shard_map(
        on_device,
        mesh=fine,
        in_specs=(tokens, tokens, P(dp, mp), P(None, mp), P(), P(None, dp), tokens),
        out_specs=(tokens, tokens, P(dp, mp), P(None, mp)),
        check_vma=False,
    )
```

```python
import math

import jax
import jax.numpy as jnp
from jax import lax
from jax.sharding import Mesh, PartitionSpec as P

XH, NY, NZ, XL, NC = 2, 4, 8, 2, 2
BF = jnp.bfloat16
F32 = jnp.float32
HIGHEST = lax.Precision.HIGHEST


def swap(a, axis):
    return lax.ppermute(a, axis, [(0, 1), (1, 0)])


def exchange(a, axis):
    return lax.all_to_all(a, axis, 0, 0, tiled=True)


def spread(a, axis, n):
    return exchange(jnp.broadcast_to(a[None], (n,) + a.shape), axis)


def pick(a, at, dim):
    return lax.dynamic_index_in_dim(a, at, dim, keepdims=False)


def in_order(index, own, other, dim):
    first = jnp.where(index == 0, own, other)
    second = jnp.where(index == 0, other, own)
    return jnp.stack([first, second], axis=dim)


def mixture(meta_graph):
    counts = meta_graph.astype(F32)
    totals = jnp.maximum(jnp.sum(counts, axis=1, keepdims=True), 1.0)
    return jnp.eye(meta_graph.shape[0], dtype=F32) + counts / totals


def members(ids, strategies):
    return (lax.broadcasted_iota(jnp.int32, (strategies, 1), 0) == ids[None, :]).astype(F32)


def rows_of(one_hot, table):
    return lax.dot_general(one_hot, table, (((0,), (0,)), ((), ())), precision=HIGHEST, preferred_element_type=F32)


def on_device(head_out, residual, out_weight, strategy_table, meta_graph, strategy_ids, cotangent):
    batches, local_rows, cols = head_out.shape
    rows, half, wide = batches * local_rows, batches * local_rows // 2, cols // 2
    strategies = meta_graph.shape[0]
    wr = out_weight.shape[0]
    pad = 16
    xh, y, xl, c = (lax.axis_index(name) for name in ("xh", "y", "xl", "c"))
    grad_scale = 1.0 / math.sqrt(rows * XH * NY * NZ)

    ho = head_out.reshape(rows, cols)
    cot = cotangent.reshape(rows, cols)
    ids = strategy_ids.reshape(rows)

    cot_parts = cot.reshape(NC, half, cols)
    other = swap(pick(cot_parts, 1 - c, 0), "c")
    mine = in_order(c, pick(cot_parts, c, 0), other, 0)
    by_y = mine.reshape(NC, half, 2, wide).transpose(0, 2, 1, 3).reshape(NY, half, wide)
    tag = pick(ids.reshape(NC, half), c, 0).astype(BF)
    tag = jnp.broadcast_to(jnp.pad(tag, (0, wide - half))[None, None], (NY, pad, wide))
    got = exchange(jnp.concatenate([by_y, tag], axis=1), "y")
    cot_y = got[:, :half].reshape(NY * half, wide)
    ids_y = got[:, half, :half].astype(jnp.int32).reshape(NY * half)

    ho_y = spread(ho, "y", NY).reshape(NY * rows, cols)

    unit = in_order(xh, out_weight, swap(out_weight, "xh"), 0)
    weight = lax.all_gather(unit, "z", axis=1, tiled=True).reshape(cols, cols)

    mixing = mixture(meta_graph)
    table = jnp.dot(mixing, strategy_table.astype(F32), precision=HIGHEST)
    there = swap(strategy_table, "c")
    owner = jnp.where(y // 2 == c, strategy_table, there).reshape(strategies, 2, wide)
    table_y = jnp.dot(mixing, pick(owner, y % 2, 1).astype(F32), precision=HIGHEST)
    hot_y = members(ids_y, strategies)
    gating_y = 1.0 + rows_of(hot_y, table_y)
    grad_y = (cot_y.astype(F32) * gating_y).astype(BF)

    both = jnp.concatenate([jnp.where(xl == 0, grad_y, far) if i == 0 else jnp.where(xl == 0, far, grad_y)
                            for i, far in enumerate([swap(grad_y, "xl")] * 2)], axis=1)
    grads = in_order(c, both.reshape(NY, half, cols), swap(both, "c").reshape(NY, half, cols), 1)
    grads = grads.reshape(NY * rows, cols)

    partial_sum = lax.dot_general(ho_y, weight, (((1,), (1,)), ((), ())), preferred_element_type=F32)
    parts = partial_sum.astype(BF).reshape(NY, NC, half, cols)
    chip = pick(parts, c, 1).astype(F32) + swap(pick(parts, 1 - c, 1), "c").astype(F32)
    chip = chip.reshape(NY * half, XL, wide)
    away = swap(pick(chip, 1 - xl, 1).astype(BF), "xl")
    projected = pick(chip, xl, 1) + away.astype(F32)

    table_part = jnp.dot(hot_y, cot_y.astype(F32) * projected, precision=HIGHEST)
    table_part = table_part.reshape(NC, strategies // NC, wide)
    table_sum = pick(table_part, c, 0) + swap(pick(table_part, 1 - c, 0), "c")
    table_sum = table_sum + swap(table_sum, "xh")
    table_sum = jnp.sum(spread(table_sum, "z", NZ), axis=0)
    table_all = spread(table_sum, "y", NY).reshape(NC, 2, strategies // NC, wide)
    rest = swap(pick(table_all, 1 - c, 0), "c")
    table_sum = in_order(c, pick(table_all, c, 0), rest, 1)
    table_sum = table_sum.reshape(2, strategies, wide).transpose(1, 0, 2).reshape(strategies, cols)
    table_grad = jnp.dot(mixing.T, table_sum, precision=HIGHEST) * grad_scale

    home = exchange(projected.astype(BF).reshape(NY, half, wide), "y")
    home = home.reshape(NC, 2, half, wide)
    back = swap(pick(home, 1 - c, 0), "c")
    proj = in_order(c, pick(home, c, 0), back, 1).reshape(2, rows, wide)
    gating = 1.0 + rows_of(members(ids, strategies), table)
    proj = jnp.concatenate([proj[0], proj[1]], axis=1).astype(F32)
    layer_out = (residual.reshape(rows, cols).astype(F32) + proj * gating).astype(BF)

    head_grad = jnp.dot(grads, weight, preferred_element_type=F32).astype(BF)
    head_grad = exchange(head_grad.reshape(NY, rows, cols), "y").astype(F32)
    head_grad = jnp.sum(head_grad, axis=0).astype(BF)

    wg = lax.dot_general(grads, ho_y, (((0,), (0,)), ((), ())), preferred_element_type=F32).astype(BF)
    wg = lax.psum_scatter(wg.reshape(XH, NZ * wr, cols), "z", scatter_dimension=1, tiled=True)
    weight_sum = pick(wg, xh, 0).astype(F32) + swap(pick(wg, 1 - xh, 0), "xh").astype(F32)

    shape = head_out.shape
    return layer_out.reshape(shape), head_grad.reshape(shape), weight_sum * grad_scale, table_grad


def solution(mesh):
    fine = Mesh(mesh.devices.reshape(XH, NY, NZ, XL, NC), ("xh", "y", "z", "xl", "c"))
    dp, mp = ("xh", "y", "z"), ("xl", "c")
    tokens = P(None, dp, mp)
    return jax.shard_map(
        on_device,
        mesh=fine,
        in_specs=(tokens, tokens, P(dp, mp), P(None, mp), P(), P(None, dp), tokens),
        out_specs=(tokens, tokens, P(dp, mp), P(None, mp)),
        check_vma=False,
    )
```

```python
import math

import jax
import jax.numpy as jnp
from jax import lax
from jax.experimental import pallas as pl
from jax.experimental.pallas import tpu as pltpu
from jax.sharding import Mesh, PartitionSpec as P

XH, NY, NZ, XL, NC = 2, 4, 8, 2, 2
BF = jnp.bfloat16
F32 = jnp.float32
HIGHEST = lax.Precision.HIGHEST


def swap(a, axis):
    return lax.ppermute(a, axis, [(0, 1), (1, 0)])


def exchange(a, axis):
    return lax.all_to_all(a, axis, 0, 0, tiled=True)


def spread(a, axis, n):
    return exchange(jnp.broadcast_to(a[None], (n,) + a.shape), axis)


def turn(a, k):
    return lax.ppermute(a, "y", [(i, (i + k) % NY) for i in range(NY)])


def gather_y(a, y):
    half = a.shape[1] // 2
    up, down = turn(a, 1), turn(a, -1)
    out = jnp.zeros((NY,) + a.shape, a.dtype)
    for piece, k in ((a, 0), (up, 1), (down, 3)):
        out = lax.dynamic_update_slice(out, piece[None], ((y - k) % NY, 0, 0))
    out = lax.dynamic_update_slice(out, turn(up[:, :half], 1)[None], ((y + 2) % NY, 0, 0))
    return lax.dynamic_update_slice(out, turn(down[:, half:], -1)[None], ((y + 2) % NY, 0, half))


def scatter_y(a, y):
    half = a.shape[2] // 2
    block = lambda k: pick(a, (y + k) % NY, 0)
    far = block(2)
    up, down = turn(far[:, :half], 1), turn(far[:, half:], -1)
    next_up, next_down = block(1), block(3)
    add = lambda p, q: (p.astype(F32) + q.astype(F32)).astype(BF)
    next_up = jnp.concatenate([add(next_up[:, :half], up), next_up[:, half:]], axis=1)
    next_down = jnp.concatenate([next_down[:, :half], add(next_down[:, half:], down)], axis=1)
    return block(0).astype(F32) + turn(next_up, 1).astype(F32) + turn(next_down, -1).astype(F32)


VMEM = pl.BlockSpec(memory_space=pltpu.VMEM)
SMEM = pl.BlockSpec(memory_space=pltpu.SMEM)
STEP = 256


def call(body, at, operands, out_shape):
    size = lambda a: math.prod(a.shape) * a.dtype.itemsize
    moved = sum(size(a) for a in operands) + size(out_shape)
    return pl.pallas_call(
        body,
        out_shape=out_shape,
        in_specs=[SMEM] + [VMEM] * len(operands),
        out_specs=VMEM,
        compiler_params=pltpu.CompilerParams(vmem_limit_bytes=32 * 2**20),
        cost_estimate=pl.CostEstimate(flops=3 * 2**30, bytes_accessed=moved, transcendentals=0),
    )(at, *operands)


def project_body(at, ho, w, out):
    rows = ho[:, at[0]].reshape(-1, ho.shape[-1])
    for x in range(XL):
        for n in range(0, w.shape[1], STEP):
            out[x, :, n : n + STEP] = lax.dot_general(
                rows, w[x, n : n + STEP, :], (((1,), (1,)), ((), ())), preferred_element_type=F32
            ).astype(BF)


def weight_body(at, near, far, near_c, far_c, ho, out):
    xl, c = at[0], at[1]
    mine = ho[:, c].reshape(-1, ho.shape[-1])
    theirs = ho[:, 1 - c].reshape(-1, ho.shape[-1])
    over = (((0,), (0,)), ((), ()))
    for x, p, q in ((xl, near, near_c), (1 - xl, far, far_c)):
        for n in range(0, out.shape[-1], STEP):
            total = lax.dot_general(p[...], mine[:, n : n + STEP], over, preferred_element_type=F32)
            total += lax.dot_general(q[...], theirs[:, n : n + STEP], over, preferred_element_type=F32)
            out[x, :, n : n + STEP] = total.astype(BF)


def head_body(at, near, far, near_c, far_c, w, out):
    xl, c = at[0], at[1]
    for half, p, q in ((c, near, far), (1 - c, near_c, far_c)):
        for n in range(0, out.shape[-1], STEP):
            total = jnp.dot(p[...], w[xl, :, n : n + STEP], preferred_element_type=F32)
            total += jnp.dot(q[...], w[1 - xl, :, n : n + STEP], preferred_element_type=F32)
            out[:, half, :, n : n + STEP] = total.astype(BF).reshape(NY, -1, STEP)


def pick(a, at, dim):
    return lax.dynamic_index_in_dim(a, at, dim, keepdims=False)


def in_order(index, own, other, dim):
    first = jnp.where(index == 0, own, other)
    second = jnp.where(index == 0, other, own)
    return jnp.stack([first, second], axis=dim)


def mixture(meta_graph):
    counts = meta_graph.astype(F32)
    totals = jnp.maximum(jnp.sum(counts, axis=1, keepdims=True), 1.0)
    return jnp.eye(meta_graph.shape[0], dtype=F32) + counts / totals


def members(ids, strategies):
    return (lax.broadcasted_iota(jnp.int32, (strategies, 1), 0) == ids[None, :]).astype(F32)


def rows_of(one_hot, table):
    return lax.dot_general(one_hot, table, (((0,), (0,)), ((), ())), precision=HIGHEST, preferred_element_type=F32)


def on_device(head_out, residual, out_weight, strategy_table, meta_graph, strategy_ids, cotangent):
    batches, local_rows, cols = head_out.shape
    rows, half, wide = batches * local_rows, batches * local_rows // 2, cols // 2
    strategies = meta_graph.shape[0]
    wr = out_weight.shape[0]
    pad = 16
    xh, y, xl, c = (lax.axis_index(name) for name in ("xh", "y", "xl", "c"))
    grad_scale = 1.0 / math.sqrt(rows * XH * NY * NZ)

    ho = head_out.reshape(rows, cols)
    cot = cotangent.reshape(rows, cols)
    ids = strategy_ids.reshape(rows)

    cot_parts = cot.reshape(NC, half, cols)
    other = swap(pick(cot_parts, 1 - c, 0), "c")
    mine = in_order(c, pick(cot_parts, c, 0), other, 0)
    by_y = mine.reshape(NC, half, 2, wide).transpose(0, 2, 1, 3).reshape(NY, half, wide)
    tag = pick(ids.reshape(NC, half), c, 0).astype(BF)
    tag = jnp.broadcast_to(jnp.pad(tag, (0, wide - half))[None, None], (NY, pad, wide))
    got = exchange(jnp.concatenate([by_y, tag], axis=1), "y")
    cot_y = got[:, :half].reshape(NY * half, wide)
    ids_y = got[:, half, :half].astype(jnp.int32).reshape(NY * half)

    ho_y = gather_y(ho, y).reshape(NY, NC, half, cols)

    unit = in_order(xh, out_weight, swap(out_weight, "xh"), 0)
    weight = lax.all_gather(unit, "z", axis=1, tiled=True)

    mixing = mixture(meta_graph)
    table = jnp.dot(mixing, strategy_table.astype(F32), precision=HIGHEST)
    there = swap(strategy_table, "c")
    owner = jnp.where(y // 2 == c, strategy_table, there).reshape(strategies, 2, wide)
    table_y = jnp.dot(mixing, pick(owner, y % 2, 1).astype(F32), precision=HIGHEST)
    hot_y = members(ids_y, strategies)
    gating_y = 1.0 + rows_of(hot_y, table_y)
    grad_y = (cot_y.astype(F32) * gating_y).astype(BF)

    far = swap(grad_y, "xl")
    pieces = (grad_y, far, swap(grad_y, "c"), swap(far, "c"))
    at = jnp.stack([xl, c]).astype(jnp.int32)

    wg = call(weight_body, at, pieces + (ho_y,), jax.ShapeDtypeStruct((XH, NZ * wr, cols), BF))
    wg = lax.psum_scatter(wg, "z", scatter_dimension=1, tiled=True)
    weight_sum = pick(wg, xh, 0).astype(F32) + swap(pick(wg, 1 - xh, 0), "xh").astype(F32)

    project = lambda core: call(
        project_body, core.reshape(1).astype(jnp.int32), (ho_y, weight), jax.ShapeDtypeStruct((XL, NY * half, wide), BF)
    )
    theirs = swap(project(1 - c), "c")
    keep = project(c)
    chip = lambda x: pick(keep, x, 0).astype(F32) + pick(theirs, x, 0).astype(F32)
    projected = chip(xl) + swap(chip(1 - xl).astype(BF), "xl").astype(F32)

    table_part = jnp.dot(hot_y, cot_y.astype(F32) * projected, precision=HIGHEST)
    table_part = table_part.reshape(NC, strategies // NC, wide)
    table_sum = pick(table_part, c, 0) + swap(pick(table_part, 1 - c, 0), "c")
    table_sum = table_sum + swap(table_sum, "xh")
    table_sum = jnp.sum(spread(table_sum.astype(BF), "z", NZ).astype(F32), axis=0)
    table_all = spread(table_sum, "y", NY).reshape(NC, 2, strategies // NC, wide)
    rest = swap(pick(table_all, 1 - c, 0), "c")
    table_sum = in_order(c, pick(table_all, c, 0), rest, 1)
    table_sum = table_sum.reshape(2, strategies, wide).transpose(1, 0, 2).reshape(strategies, cols)
    table_grad = jnp.dot(mixing.T, table_sum, precision=HIGHEST) * grad_scale

    home = exchange(projected.astype(BF).reshape(NY, half, wide), "y")
    home = home.reshape(NC, 2, half, wide)
    back = swap(pick(home, 1 - c, 0), "c")
    proj = in_order(c, pick(home, c, 0), back, 1).reshape(2, rows, wide)
    gating = 1.0 + rows_of(members(ids, strategies), table)
    proj = jnp.concatenate([proj[0], proj[1]], axis=1).astype(F32)
    layer_out = (residual.reshape(rows, cols).astype(F32) + proj * gating).astype(BF)

    head_grad = call(head_body, at, pieces + (weight,), jax.ShapeDtypeStruct((NY, NC, half, cols), BF))
    head_grad = scatter_y(head_grad.reshape(NY, rows, cols), y).astype(BF)

    shape = head_out.shape
    return layer_out.reshape(shape), head_grad.reshape(shape), weight_sum * grad_scale, table_grad


def solution(mesh):
    fine = Mesh(mesh.devices.reshape(XH, NY, NZ, XL, NC), ("xh", "y", "z", "xl", "c"))
    dp, mp = ("xh", "y", "z"), ("xl", "c")
    tokens = P(None, dp, mp)
    return jax.shard_map(
        on_device,
        mesh=fine,
        in_specs=(tokens, tokens, P(dp, mp), P(None, mp), P(), P(None, dp), tokens),
        out_specs=(tokens, tokens, P(dp, mp), P(None, mp)),
        check_vma=False,
    )
```

```python
import math

import jax
import jax.numpy as jnp
from jax import lax
from jax.experimental import pallas as pl
from jax.experimental.pallas import tpu as pltpu
from jax.sharding import Mesh, PartitionSpec as P

XH, NY, NZ, XL, NC = 2, 4, 8, 2, 2
BF = jnp.bfloat16
F32 = jnp.float32
HIGHEST = lax.Precision.HIGHEST


def swap(a, axis):
    return lax.ppermute(a, axis, [(0, 1), (1, 0)])


def exchange(a, axis):
    return lax.all_to_all(a, axis, 0, 0, tiled=True)


def spread(a, axis, n):
    return exchange(jnp.broadcast_to(a[None], (n,) + a.shape), axis)


def turn(a, k):
    return lax.ppermute(a, "y", [(i, (i + k) % NY) for i in range(NY)])


def gather_y(a, y, after):
    at_none = y.reshape(1).astype(jnp.int32)
    half = a.shape[1] // 2
    sent = call(copy_body, at_none, (a,), jax.ShapeDtypeStruct(a.shape, a.dtype), after)
    up, down = turn(sent, 1), turn(sent, -1)
    out = jnp.zeros((NY,) + a.shape, a.dtype)
    for piece, k in ((a, 0), (up, 1), (down, 3)):
        out = lax.dynamic_update_slice(out, piece[None], ((y - k) % NY, 0, 0))
    out = lax.dynamic_update_slice(out, turn(up[:, :half], 1)[None], ((y + 2) % NY, 0, 0))
    return lax.dynamic_update_slice(out, turn(down[:, half:], -1)[None], ((y + 2) % NY, 0, half))


def scatter_y(a, y):
    half = a.shape[2] // 2
    block = lambda k: pick(a, (y + k) % NY, 0)
    far = block(2)
    up, down = turn(far[:, :half], 1), turn(far[:, half:], -1)
    next_up, next_down = block(1), block(3)
    add = lambda p, q: (p.astype(F32) + q.astype(F32)).astype(BF)
    next_up = jnp.concatenate([add(next_up[:, :half], up), next_up[:, half:]], axis=1)
    next_down = jnp.concatenate([next_down[:, :half], add(next_down[:, half:], down)], axis=1)
    return block(0).astype(F32) + turn(next_up, 1).astype(F32) + turn(next_down, -1).astype(F32)


VMEM = pl.BlockSpec(memory_space=pltpu.VMEM)
SMEM = pl.BlockSpec(memory_space=pltpu.SMEM)
STEP = 256


def call(body, at, operands, out_shape, after=()):
    size = lambda a: math.prod(a.shape) * a.dtype.itemsize
    moved = sum(size(a) for a in operands) + size(out_shape)
    return pl.pallas_call(
        lambda *refs: body(*refs[: len(operands) + 1], refs[-1]),
        out_shape=out_shape,
        in_specs=[SMEM] + [VMEM] * len(operands) + [pl.BlockSpec(memory_space=pl.ANY)] * len(after),
        out_specs=VMEM,
        compiler_params=pltpu.CompilerParams(vmem_limit_bytes=32 * 2**20),
        cost_estimate=pl.CostEstimate(flops=3 * 2**30, bytes_accessed=moved, transcendentals=0),
    )(at, *operands, *after)


def copy_body(at, a, out):
    out[...] = a[...]


def add_body(at, a, b, out):
    out[...] = a[...].astype(F32) + b[...].astype(F32)


def pair_body(at, own, other, out):
    out[at[0]] = own[...]
    out[1 - at[0]] = other[...]


def project_body(at, ho, w, out):
    rows = ho[:, at[0]].reshape(-1, ho.shape[-1])
    for x in range(XL):
        for n in range(0, w.shape[1], STEP):
            out[x, :, n : n + STEP] = lax.dot_general(
                rows, w[x, n : n + STEP, :], (((1,), (1,)), ((), ())), preferred_element_type=F32
            ).astype(BF)


def weight_body(at, near, far, near_c, far_c, ho, out):
    xl, c = at[0], at[1]
    mine = ho[:, c].reshape(-1, ho.shape[-1])
    theirs = ho[:, 1 - c].reshape(-1, ho.shape[-1])
    over = (((0,), (0,)), ((), ()))
    for x, p, q in ((xl, near, near_c), (1 - xl, far, far_c)):
        for n in range(0, out.shape[-1], STEP):
            total = lax.dot_general(p[...], mine[:, n : n + STEP], over, preferred_element_type=F32)
            total += lax.dot_general(q[...], theirs[:, n : n + STEP], over, preferred_element_type=F32)
            out[x, :, n : n + STEP] = total.astype(BF)


def head_body(at, near, far, near_c, far_c, w, out):
    xl, c = at[0], at[1]
    for half, p, q in ((c, near, far), (1 - c, near_c, far_c)):
        for n in range(0, out.shape[-1], STEP):
            total = jnp.dot(p[...], w[xl, :, n : n + STEP], preferred_element_type=F32)
            total += jnp.dot(q[...], w[1 - xl, :, n : n + STEP], preferred_element_type=F32)
            out[:, half, :, n : n + STEP] = total.astype(BF).reshape(NY, -1, STEP)


def pick(a, at, dim):
    return lax.dynamic_index_in_dim(a, at, dim, keepdims=False)


def in_order(index, own, other, dim):
    first = jnp.where(index == 0, own, other)
    second = jnp.where(index == 0, other, own)
    return jnp.stack([first, second], axis=dim)


def mixture(meta_graph):
    counts = meta_graph.astype(F32)
    totals = jnp.maximum(jnp.sum(counts, axis=1, keepdims=True), 1.0)
    return jnp.eye(meta_graph.shape[0], dtype=F32) + counts / totals


def members(ids, strategies):
    return (lax.broadcasted_iota(jnp.int32, (strategies, 1), 0) == ids[None, :]).astype(F32)


def rows_of(one_hot, table):
    return lax.dot_general(one_hot, table, (((0,), (0,)), ((), ())), precision=HIGHEST, preferred_element_type=F32)


def on_device(head_out, residual, out_weight, strategy_table, meta_graph, strategy_ids, cotangent):
    batches, local_rows, cols = head_out.shape
    rows, half, wide = batches * local_rows, batches * local_rows // 2, cols // 2
    strategies = meta_graph.shape[0]
    wr = out_weight.shape[0]
    pad = 16
    xh, y, xl, c = (lax.axis_index(name) for name in ("xh", "y", "xl", "c"))
    grad_scale = 1.0 / math.sqrt(rows * XH * NY * NZ)

    ho = head_out.reshape(rows, cols)
    cot = cotangent.reshape(rows, cols)
    ids = strategy_ids.reshape(rows)

    cot_parts = cot.reshape(NC, half, cols)
    other = swap(pick(cot_parts, 1 - c, 0), "c")
    mine = in_order(c, pick(cot_parts, c, 0), other, 0)
    by_y = mine.reshape(NC, half, 2, wide).transpose(0, 2, 1, 3).reshape(NY, half, wide)
    tag = pick(ids.reshape(NC, half), c, 0).astype(BF)
    tag = jnp.broadcast_to(jnp.pad(tag, (0, wide - half))[None, None], (NY, pad, wide))
    got = exchange(jnp.concatenate([by_y, tag], axis=1), "y")
    cot_y = got[:, :half].reshape(NY * half, wide)
    ids_y = got[:, half, :half].astype(jnp.int32).reshape(NY * half)

    ho_y = gather_y(ho, y, (got,)).reshape(NY, NC, half, cols)

    unit = call(
        pair_body,
        xh.reshape(1).astype(jnp.int32),
        (out_weight, swap(out_weight, "xh")),
        jax.ShapeDtypeStruct((XH,) + out_weight.shape, BF),
        (other,),
    )
    weight = lax.all_gather(unit, "z", axis=1, tiled=True)

    mixing = mixture(meta_graph)
    table = jnp.dot(mixing, strategy_table.astype(F32), precision=HIGHEST)
    there = swap(strategy_table, "c")
    owner = jnp.where(y // 2 == c, strategy_table, there).reshape(strategies, 2, wide)
    table_y = jnp.dot(mixing, pick(owner, y % 2, 1).astype(F32), precision=HIGHEST)
    hot_y = members(ids_y, strategies)
    gating_y = 1.0 + rows_of(hot_y, table_y)
    grad_y = (cot_y.astype(F32) * gating_y).astype(BF)

    far = swap(grad_y, "xl")
    pieces = (grad_y, far, swap(grad_y, "c"), swap(far, "c"))
    at = jnp.stack([xl, c]).astype(jnp.int32)

    project = lambda core, after: call(
        project_body, core.reshape(1).astype(jnp.int32), (ho_y, weight), jax.ShapeDtypeStruct((XL, NY * half, wide), BF), after
    )
    theirs = swap(project(1 - c, ()), "c")
    keep = project(c, ())
    chip = lambda x: pick(keep, x, 0).astype(F32) + pick(theirs, x, 0).astype(F32)
    projected = chip(xl) + swap(chip(1 - xl).astype(BF), "xl").astype(F32)

    wg = call(weight_body, at, pieces + (ho_y,), jax.ShapeDtypeStruct((XH, NZ * wr, cols), BF))
    wg_part = lax.psum_scatter(wg, "z", scatter_dimension=1, tiled=True)
    weight_sum = pick(wg_part, xh, 0).astype(F32) + swap(pick(wg_part, 1 - xh, 0), "xh").astype(F32)

    home = exchange(projected.astype(BF).reshape(NY, half, wide), "y")
    table_part = jnp.dot(hot_y, cot_y.astype(F32) * projected, precision=HIGHEST)
    table_part = table_part.reshape(NC, strategies // NC, wide)
    table_sum = pick(table_part, c, 0) + swap(pick(table_part, 1 - c, 0), "c")
    table_sum = table_sum + swap(table_sum, "xh")
    for bit in (1, 2, 4):
        sent = table_sum.astype(BF)
        far_sum = lax.ppermute(sent, "z", [(i, i ^ bit) for i in range(NZ)])
        if bit < 4:
            table_sum = sent.astype(F32) + far_sum.astype(F32)
        else:
            table_sum = call(add_body, at, (sent, far_sum), jax.ShapeDtypeStruct(sent.shape, F32), (home,))
    table_all = spread(table_sum, "y", NY).reshape(NC, 2, strategies // NC, wide)
    rest = swap(pick(table_all, 1 - c, 0), "c")
    table_sum = in_order(c, pick(table_all, c, 0), rest, 1)
    table_sum = table_sum.reshape(2, strategies, wide).transpose(1, 0, 2).reshape(strategies, cols)
    table_grad = jnp.dot(mixing.T, table_sum, precision=HIGHEST) * grad_scale

    parts = home.reshape(NC, 2, half, wide)
    back = swap(pick(parts, 1 - c, 0), "c")
    proj = in_order(c, pick(parts, c, 0), back, 1).reshape(2, rows, wide)
    gating = 1.0 + rows_of(members(ids, strategies), table)
    proj = jnp.concatenate([proj[0], proj[1]], axis=1).astype(F32)
    layer_out = (residual.reshape(rows, cols).astype(F32) + proj * gating).astype(BF)

    head_grad = call(head_body, at, pieces + (weight,), jax.ShapeDtypeStruct((NY, NC, half, cols), BF), (keep,))
    head_grad = scatter_y(head_grad.reshape(NY, rows, cols), y).astype(BF)

    shape = head_out.shape
    return layer_out.reshape(shape), head_grad.reshape(shape), weight_sum * grad_scale, table_grad


def solution(mesh):
    fine = Mesh(mesh.devices.reshape(XH, NY, NZ, XL, NC), ("xh", "y", "z", "xl", "c"))
    dp, mp = ("xh", "y", "z"), ("xl", "c")
    tokens = P(None, dp, mp)
    return jax.shard_map(
        on_device,
        mesh=fine,
        in_specs=(tokens, tokens, P(dp, mp), P(None, mp), P(), P(None, dp), tokens),
        out_specs=(tokens, tokens, P(dp, mp), P(None, mp)),
        check_vma=False,
    )
```

```python
import math

import jax
import jax.numpy as jnp
from jax import lax
from jax.experimental import pallas as pl
from jax.experimental.pallas import tpu as pltpu
from jax.sharding import Mesh, PartitionSpec as P

XH, NY, NZ, XL, NC = 2, 4, 8, 2, 2
BF = jnp.bfloat16
F32 = jnp.float32
HIGHEST = lax.Precision.HIGHEST


def swap(a, axis):
    return lax.ppermute(a, axis, [(0, 1), (1, 0)])


def exchange(a, axis):
    return lax.all_to_all(a, axis, 0, 0, tiled=True)


def spread(a, axis, n):
    return exchange(jnp.broadcast_to(a[None], (n,) + a.shape), axis)


def turn(a, k):
    return lax.ppermute(a, "y", [(i, (i + k) % NY) for i in range(NY)])


def gather_y(a, y, first):
    half, head = a.shape[1] // 2, first[0].shape[0]
    up = jnp.concatenate([first[0], turn(a[head:], 1)], axis=0)
    down = jnp.concatenate([first[1], turn(a[head:], -1)], axis=0)
    out = jnp.zeros((NY,) + a.shape, a.dtype)
    for piece, k in ((a, 0), (up, 1), (down, 3)):
        out = lax.dynamic_update_slice(out, piece[None], ((y - k) % NY, 0, 0))
    out = lax.dynamic_update_slice(out, turn(up[:, :half], 1)[None], ((y + 2) % NY, 0, 0))
    return lax.dynamic_update_slice(out, turn(down[:, half:], -1)[None], ((y + 2) % NY, 0, half))


def far_blocks(a, y):
    half = a.shape[2] // 2
    far = pick(a, (y + 2) % NY, 0)
    return turn(far[:, :half], 1), turn(far[:, half:], -1)


def scatter_y(a, far, y):
    block = jax.ShapeDtypeStruct(a.shape[1:], BF)
    up, down = call(pass_body, y.reshape(1).astype(jnp.int32), (a,) + far, (block, block))
    return pick(a, y, 0).astype(F32) + turn(up, 1).astype(F32) + turn(down, -1).astype(F32)


VMEM = pl.BlockSpec(memory_space=pltpu.VMEM)
SMEM = pl.BlockSpec(memory_space=pltpu.SMEM)
STEP = 256


def call(body, at, operands, out_shape, after=()):
    count = len(operands) + 1
    return pl.pallas_call(
        lambda *refs: body(*refs[:count], *refs[count + len(after) :]),
        out_shape=out_shape,
        in_specs=[SMEM] + [VMEM] * len(operands) + [pl.BlockSpec(memory_space=pl.ANY)] * len(after),
        out_specs=jax.tree.map(lambda _: VMEM, out_shape),
        compiler_params=pltpu.CompilerParams(vmem_limit_bytes=16 * 2**20),
        cost_estimate=pl.CostEstimate(flops=2**20, bytes_accessed=2**10, transcendentals=0),
    )(at, *operands, *after)


def pass_body(at, a, from_below, from_above, up, down):
    half = from_below.shape[1]
    above, below = lax.rem(at[0] + 1, NY), lax.rem(at[0] + NY - 1, NY)
    up[:, :half] = (a[above, :, :half].astype(F32) + from_below[...].astype(F32)).astype(BF)
    up[:, half:] = a[above, :, half:]
    down[:, :half] = a[below, :, :half]
    down[:, half:] = (a[below, :, half:].astype(F32) + from_above[...].astype(F32)).astype(BF)


def take_body(at, a, out):
    out[...] = a[at[0]]


def add_body(at, a, b, out):
    out[...] = a[...].astype(F32) + b[...].astype(F32)


def pair_body(at, own, other, out):
    out[at[0]] = own[...]
    out[1 - at[0]] = other[...]


def merge_body(at, keep, theirs, away, cot, hot, home, table):
    x = at[0]
    projected = keep[x].astype(F32) + theirs[x].astype(F32) + away[...].astype(F32)
    home[...] = projected.astype(BF)
    rest = cot[...].astype(F32) * projected
    total = jnp.zeros(table.shape, F32)
    for _ in range(3):
        part = rest.astype(BF)
        total += jnp.dot(hot[...], part, preferred_element_type=F32)
        rest = rest - part.astype(F32)
    table[...] = total


def project_body(at, ho, w, out):
    rows = ho[:, at[0]].reshape(-1, ho.shape[-1])
    for x in range(XL):
        for n in range(0, w.shape[1], STEP):
            out[x, :, n : n + STEP] = lax.dot_general(
                rows, w[x, n : n + STEP, :], (((1,), (1,)), ((), ())), preferred_element_type=F32
            ).astype(BF)


def weight_body(at, near, far, near_c, far_c, ho, out):
    xl, c = at[0], at[1]
    mine = ho[:, c].reshape(-1, ho.shape[-1])
    theirs = ho[:, 1 - c].reshape(-1, ho.shape[-1])
    over = (((0,), (0,)), ((), ()))
    for x, p, q in ((xl, near, near_c), (1 - xl, far, far_c)):
        for n in range(0, out.shape[-1], STEP):
            total = lax.dot_general(p[...], mine[:, n : n + STEP], over, preferred_element_type=F32)
            total += lax.dot_general(q[...], theirs[:, n : n + STEP], over, preferred_element_type=F32)
            out[x, :, n : n + STEP] = total.astype(BF)


def head_body(at, near, far, near_c, far_c, w, out):
    xl, c = at[0], at[1]
    for half, p, q in ((c, near, far), (1 - c, near_c, far_c)):
        for n in range(0, out.shape[-1], STEP):
            total = jnp.dot(p[...], w[xl, :, n : n + STEP], preferred_element_type=F32)
            total += jnp.dot(q[...], w[1 - xl, :, n : n + STEP], preferred_element_type=F32)
            out[:, half, :, n : n + STEP] = total.astype(BF).reshape(NY, -1, STEP)


def pick(a, at, dim):
    return lax.dynamic_index_in_dim(a, at, dim, keepdims=False)


def in_order(index, own, other, dim):
    first = jnp.where(index == 0, own, other)
    second = jnp.where(index == 0, other, own)
    return jnp.stack([first, second], axis=dim)


def mixture(meta_graph):
    counts = meta_graph.astype(F32)
    totals = jnp.maximum(jnp.sum(counts, axis=1, keepdims=True), 1.0)
    return jnp.eye(meta_graph.shape[0], dtype=F32) + counts / totals


def members(ids, strategies):
    return (lax.broadcasted_iota(jnp.int32, (strategies, 1), 0) == ids[None, :]).astype(F32)


def rows_of(one_hot, table):
    return lax.dot_general(one_hot, table, (((0,), (0,)), ((), ())), precision=HIGHEST, preferred_element_type=F32)


def on_device(head_out, residual, out_weight, strategy_table, meta_graph, strategy_ids, cotangent):
    batches, local_rows, cols = head_out.shape
    rows, half, wide = batches * local_rows, batches * local_rows // 2, cols // 2
    strategies = meta_graph.shape[0]
    wr = out_weight.shape[0]
    pad = 16
    xh, y, xl, c = (lax.axis_index(name) for name in ("xh", "y", "xl", "c"))
    grad_scale = 1.0 / math.sqrt(rows * XH * NY * NZ)

    ho = head_out.reshape(rows, cols)
    cot = cotangent.reshape(rows, cols)
    ids = strategy_ids.reshape(rows)

    first = turn(ho[: rows // 4], 1), turn(ho[: rows // 4], -1)

    cot_parts = cot.reshape(NC, half, cols)
    other = swap(pick(cot_parts, 1 - c, 0), "c")
    mine = in_order(c, pick(cot_parts, c, 0), other, 0)
    by_y = mine.reshape(NC, half, 2, wide).transpose(0, 2, 1, 3).reshape(NY, half, wide)
    tag = pick(ids.reshape(NC, half), c, 0).astype(BF)
    tag = jnp.broadcast_to(jnp.pad(tag, (0, wide - half))[None, None], (NY, pad, wide))
    got = exchange(jnp.concatenate([by_y, tag], axis=1), "y")
    cot_y = got[:, :half].reshape(NY * half, wide)
    ids_y = got[:, half, :half].astype(jnp.int32).reshape(NY * half)

    ho_y = gather_y(ho, y, first).reshape(NY, NC, half, cols)

    unit = call(
        pair_body,
        xh.reshape(1).astype(jnp.int32),
        (out_weight, swap(out_weight, "xh")),
        jax.ShapeDtypeStruct((XH,) + out_weight.shape, BF),
        (other,) + first,
    )
    weight = lax.all_gather(unit, "z", axis=1, tiled=True)

    mixing = mixture(meta_graph)
    table = jnp.dot(mixing, strategy_table.astype(F32), precision=HIGHEST)
    there = swap(strategy_table, "c")
    owner = jnp.where(y // 2 == c, strategy_table, there).reshape(strategies, 2, wide)
    table_y = jnp.dot(mixing, pick(owner, y % 2, 1).astype(F32), precision=HIGHEST)
    hot_y = members(ids_y, strategies)
    gating_y = 1.0 + rows_of(hot_y, table_y)
    grad_y = (cot_y.astype(F32) * gating_y).astype(BF)

    far = swap(grad_y, "xl")
    pieces = (grad_y, far, swap(grad_y, "c"), swap(far, "c"))
    at = jnp.stack([xl, c]).astype(jnp.int32)

    project = lambda core, after: call(
        project_body, core.reshape(1).astype(jnp.int32), (ho_y, weight), jax.ShapeDtypeStruct((XL, NY * half, wide), BF), after
    )
    theirs = swap(project(1 - c, (far,)), "c")
    keep = project(c, ())
    chip = lambda x: pick(keep, x, 0).astype(F32) + pick(theirs, x, 0).astype(F32)
    away = chip(1 - xl).astype(BF)
    wg = call(weight_body, at, pieces + (ho_y,), jax.ShapeDtypeStruct((XH, NZ * wr, cols), BF), (away,))
    head_grad = call(head_body, at, pieces + (weight,), jax.ShapeDtypeStruct((NY, NC, half, cols), BF), (wg,))
    head_grad = head_grad.reshape(NY, rows, cols)
    head_far = far_blocks(head_grad, y)
    home, table_part = call(
        merge_body,
        at,
        (keep, theirs, swap(away, "xl"), cot_y, hot_y.astype(BF)),
        (jax.ShapeDtypeStruct(away.shape, BF), jax.ShapeDtypeStruct((strategies, wide), F32)),
        head_far,
    )

    wg_part = lax.psum_scatter(wg, "z", scatter_dimension=1, tiled=True)
    wg_other = swap(pick(wg_part, 1 - xh, 0), "xh")
    weight_sum = pick(wg_part, xh, 0).astype(F32) + wg_other.astype(F32)

    home = exchange(home.reshape(NY, half, wide), "y")
    table_part = table_part.reshape(NC, strategies // NC, wide)
    table_sum = pick(table_part, c, 0) + swap(pick(table_part, 1 - c, 0), "c")
    table_sum = table_sum + swap(table_sum, "xh")
    for bit in (1, 2, 4):
        sent = table_sum.astype(BF)
        far_sum = lax.ppermute(sent, "z", [(i, i ^ bit) for i in range(NZ)])
        if bit < 4:
            table_sum = sent.astype(F32) + far_sum.astype(F32)
        else:
            table_sum = call(add_body, at, (sent, far_sum), jax.ShapeDtypeStruct(sent.shape, F32), (home,))
    table_all = spread(table_sum, "y", NY).reshape(NC, 2, strategies // NC, wide)
    rest = jax.ShapeDtypeStruct(table_all.shape[1:], F32)
    rest = swap(call(take_body, (1 - c).reshape(1).astype(jnp.int32), (table_all,), rest, (wg_other,)), "c")
    table_sum = in_order(c, pick(table_all, c, 0), rest, 1)
    table_sum = table_sum.reshape(2, strategies, wide).transpose(1, 0, 2).reshape(strategies, cols)
    table_grad = jnp.dot(mixing.T, table_sum, precision=HIGHEST) * grad_scale

    parts = home.reshape(NC, 2, half, wide)
    back = swap(pick(parts, 1 - c, 0), "c")
    proj = in_order(c, pick(parts, c, 0), back, 1).reshape(2, rows, wide)
    gating = 1.0 + rows_of(members(ids, strategies), table)
    proj = jnp.concatenate([proj[0], proj[1]], axis=1).astype(F32)
    layer_out = (residual.reshape(rows, cols).astype(F32) + proj * gating).astype(BF)

    head_grad = scatter_y(head_grad, head_far, y).astype(BF)

    shape = head_out.shape
    return layer_out.reshape(shape), head_grad.reshape(shape), weight_sum * grad_scale, table_grad


def solution(mesh):
    fine = Mesh(mesh.devices.reshape(XH, NY, NZ, XL, NC), ("xh", "y", "z", "xl", "c"))
    dp, mp = ("xh", "y", "z"), ("xl", "c")
    tokens = P(None, dp, mp)
    return jax.shard_map(
        on_device,
        mesh=fine,
        in_specs=(tokens, tokens, P(dp, mp), P(None, mp), P(), P(None, dp), tokens),
        out_specs=(tokens, tokens, P(dp, mp), P(None, mp)),
        check_vma=False,
    )
```

```python
import math

import jax
import jax.numpy as jnp
from jax import lax
from jax.experimental import pallas as pl
from jax.experimental.pallas import tpu as pltpu
from jax.sharding import Mesh, PartitionSpec as P

XH, NY, NZ, XL, NC = 2, 4, 8, 2, 2
BF = jnp.bfloat16
F32 = jnp.float32
HIGHEST = lax.Precision.HIGHEST


def swap(a, axis):
    return lax.ppermute(a, axis, [(0, 1), (1, 0)])


def exchange(a, axis):
    return lax.all_to_all(a, axis, 0, 0, tiled=True)


def spread(a, axis, n):
    return exchange(jnp.broadcast_to(a[None], (n,) + a.shape), axis)


def turn(a, k):
    return lax.ppermute(a, "y", [(i, (i + k) % NY) for i in range(NY)])


def gather_y(a, y):
    half = a.shape[1] // 2
    up, down = turn(a, 1), turn(a, -1)
    out = jnp.zeros((NY,) + a.shape, a.dtype)
    for piece, k in ((a, 0), (up, 1), (down, 3)):
        out = lax.dynamic_update_slice(out, piece[None], ((y - k) % NY, 0, 0))
    out = lax.dynamic_update_slice(out, turn(up[:, :half], 1)[None], ((y + 2) % NY, 0, 0))
    return lax.dynamic_update_slice(out, turn(down[:, half:], -1)[None], ((y + 2) % NY, 0, half))


def far_blocks(a, y):
    half = a.shape[2] // 2
    far = pick(a, (y + 2) % NY, 0)
    return turn(far[:, :half], 1), turn(far[:, half:], -1)


def scatter_y(a, far, y, after):
    block = jax.ShapeDtypeStruct(a.shape[1:], BF)
    up, down = call(pass_body, y.reshape(1).astype(jnp.int32), (a,) + far, (block, block), after)
    return pick(a, y, 0).astype(F32) + turn(up, 1).astype(F32) + turn(down, -1).astype(F32)


VMEM = pl.BlockSpec(memory_space=pltpu.VMEM)
SMEM = pl.BlockSpec(memory_space=pltpu.SMEM)
STEP = 256


def call(body, at, operands, out_shape, after=()):
    count = len(operands) + 1
    return pl.pallas_call(
        lambda *refs: body(*refs[:count], *refs[count + len(after) :]),
        out_shape=out_shape,
        in_specs=[SMEM] + [VMEM] * len(operands) + [pl.BlockSpec(memory_space=pl.ANY)] * len(after),
        out_specs=jax.tree.map(lambda _: VMEM, out_shape),
        compiler_params=pltpu.CompilerParams(vmem_limit_bytes=16 * 2**20),
        cost_estimate=pl.CostEstimate(flops=2**20, bytes_accessed=2**10, transcendentals=0),
    )(at, *operands, *after)


def pass_body(at, a, from_below, from_above, up, down):
    half = from_below.shape[1]
    above, below = lax.rem(at[0] + 1, NY), lax.rem(at[0] + NY - 1, NY)
    up[:, :half] = (a[above, :, :half].astype(F32) + from_below[...].astype(F32)).astype(BF)
    up[:, half:] = a[above, :, half:]
    down[:, :half] = a[below, :, :half]
    down[:, half:] = (a[below, :, half:].astype(F32) + from_above[...].astype(F32)).astype(BF)


def take_body(at, a, out):
    out[...] = a[at[0]]


def add_body(at, a, b, out):
    out[...] = a[...].astype(F32) + b[...].astype(F32)


def pair_body(at, own, other, out):
    out[at[0]] = own[...]
    out[1 - at[0]] = other[...]


def split3(a):
    parts = []
    for _ in range(3):
        parts.append(a.astype(BF))
        a = a - parts[-1].astype(F32)
    return parts


def hot_of(got, k, rows, strategies):
    ids = got[k, rows : rows + 16, :].astype(F32)[:1, :rows]
    return (lax.broadcasted_iota(jnp.int32, (strategies, rows), 0).astype(F32) == ids).astype(BF)


def table_body(at, mixing, own, there, out):
    where = pl.ds(pl.multiple_of(at[1] * out.shape[1], 128), out.shape[1])
    table = jnp.where(at[0] == 1, own[:, where].astype(F32), there[:, where].astype(F32))
    out[...] = jnp.dot(mixing[...], table, precision=HIGHEST, preferred_element_type=F32)


def gate_body(at, got, table, out):
    rows = out.shape[0] // NY
    parts = split3(table[...])
    for k in range(NY):
        hot = hot_of(got, k, rows, table.shape[0])
        gating = jnp.ones((rows, out.shape[1]), F32)
        for part in reversed(parts):
            gating += lax.dot_general(hot, part, (((0,), (0,)), ((), ())), preferred_element_type=F32)
        out[k * rows : (k + 1) * rows, :] = (got[k, :rows, :].astype(F32) * gating).astype(BF)


def merge_body(at, keep, theirs, away, got, home, table):
    x, rows = at[0], home.shape[0] // NY
    total = jnp.zeros(table.shape, F32)
    for k in range(NY):
        span = slice(k * rows, (k + 1) * rows)
        projected = keep[x, span, :].astype(F32) + theirs[x, span, :].astype(F32) + away[span, :].astype(F32)
        home[span, :] = projected.astype(BF)
        hot = hot_of(got, k, rows, table.shape[0])
        for part in split3(got[k, :rows, :].astype(F32) * projected):
            total += jnp.dot(hot, part, preferred_element_type=F32)
    table[...] = total


def project_body(at, ho, w, out):
    rows = ho[:, at[0]].reshape(-1, ho.shape[-1])
    for x in range(XL):
        for n in range(0, w.shape[1], STEP):
            out[x, :, n : n + STEP] = lax.dot_general(
                rows, w[x, n : n + STEP, :], (((1,), (1,)), ((), ())), preferred_element_type=F32
            ).astype(BF)


def weight_body(at, near, far, near_c, far_c, ho, out):
    xl, c = at[0], at[1]
    mine = ho[:, c].reshape(-1, ho.shape[-1])
    theirs = ho[:, 1 - c].reshape(-1, ho.shape[-1])
    over = (((0,), (0,)), ((), ()))
    for x, p, q in ((xl, near, near_c), (1 - xl, far, far_c)):
        for n in range(0, out.shape[-1], STEP):
            total = lax.dot_general(p[...], mine[:, n : n + STEP], over, preferred_element_type=F32)
            total += lax.dot_general(q[...], theirs[:, n : n + STEP], over, preferred_element_type=F32)
            out[x, :, n : n + STEP] = total.astype(BF)


def head_body(at, near, far, near_c, far_c, w, out):
    xl, c = at[0], at[1]
    for half, p, q in ((c, near, far), (1 - c, near_c, far_c)):
        for n in range(0, out.shape[-1], STEP):
            total = jnp.dot(p[...], w[xl, :, n : n + STEP], preferred_element_type=F32)
            total += jnp.dot(q[...], w[1 - xl, :, n : n + STEP], preferred_element_type=F32)
            out[:, half, :, n : n + STEP] = total.astype(BF).reshape(NY, -1, STEP)


def pick(a, at, dim):
    return lax.dynamic_index_in_dim(a, at, dim, keepdims=False)


def in_order(index, own, other, dim):
    first = jnp.where(index == 0, own, other)
    second = jnp.where(index == 0, other, own)
    return jnp.stack([first, second], axis=dim)


def mixture(meta_graph):
    counts = meta_graph.astype(F32)
    totals = jnp.maximum(jnp.sum(counts, axis=1, keepdims=True), 1.0)
    return jnp.eye(meta_graph.shape[0], dtype=F32) + counts / totals


def members(ids, strategies):
    return (lax.broadcasted_iota(jnp.int32, (strategies, 1), 0) == ids[None, :]).astype(F32)


def rows_of(one_hot, table):
    return lax.dot_general(one_hot, table, (((0,), (0,)), ((), ())), precision=HIGHEST, preferred_element_type=F32)


def on_device(head_out, residual, out_weight, strategy_table, meta_graph, strategy_ids, cotangent):
    batches, local_rows, cols = head_out.shape
    rows, half, wide = batches * local_rows, batches * local_rows // 2, cols // 2
    strategies = meta_graph.shape[0]
    wr = out_weight.shape[0]
    pad = 16
    xh, y, xl, c = (lax.axis_index(name) for name in ("xh", "y", "xl", "c"))
    grad_scale = 1.0 / math.sqrt(rows * XH * NY * NZ)

    ho = head_out.reshape(rows, cols)
    cot = cotangent.reshape(rows, cols)
    ids = strategy_ids.reshape(rows)

    cot_parts = cot.reshape(NC, half, cols)
    other = swap(pick(cot_parts, 1 - c, 0), "c")
    mine = in_order(c, pick(cot_parts, c, 0), other, 0)
    by_y = mine.reshape(NC, half, 2, wide).transpose(0, 2, 1, 3).reshape(NY, half, wide)
    tag = pick(ids.reshape(NC, half), c, 0).astype(BF)
    tag = jnp.broadcast_to(jnp.pad(tag, (0, wide - half))[None, None], (NY, pad, wide))
    got = exchange(jnp.concatenate([by_y, tag], axis=1), "y")

    ho_y = gather_y(ho, y).reshape(NY, NC, half, cols)

    unit = call(
        pair_body,
        xh.reshape(1).astype(jnp.int32),
        (out_weight, swap(out_weight, "xh")),
        jax.ShapeDtypeStruct((XH,) + out_weight.shape, BF),
        (other,),
    )
    weight = lax.all_gather(unit, "z", axis=1, tiled=True)

    mixing = mixture(meta_graph)
    table = jnp.dot(mixing, strategy_table.astype(F32), precision=HIGHEST)
    there = swap(strategy_table, "c")
    source = jnp.stack([(y // 2 == c).astype(jnp.int32), (y % 2).astype(jnp.int32)])
    table_y = call(table_body, source, (mixing, strategy_table, there), jax.ShapeDtypeStruct((strategies, wide), F32))
    grad_y = call(gate_body, source, (got, table_y), jax.ShapeDtypeStruct((NY * half, wide), BF))

    far = swap(grad_y, "xl")
    pieces = (grad_y, far, swap(grad_y, "c"), swap(far, "c"))
    at = jnp.stack([xl, c]).astype(jnp.int32)

    project = lambda core, after: call(
        project_body, core.reshape(1).astype(jnp.int32), (ho_y, weight), jax.ShapeDtypeStruct((XL, NY * half, wide), BF), after
    )
    theirs = swap(project(1 - c, (far,)), "c")
    keep = project(c, ())
    chip = lambda x: pick(keep, x, 0).astype(F32) + pick(theirs, x, 0).astype(F32)
    away = chip(1 - xl).astype(BF)
    wg = call(weight_body, at, pieces + (ho_y,), jax.ShapeDtypeStruct((XH, NZ * wr, cols), BF), (away,))
    head_grad = call(head_body, at, pieces + (weight,), jax.ShapeDtypeStruct((NY, NC, half, cols), BF), (wg,))
    head_grad = head_grad.reshape(NY, rows, cols)
    head_far = far_blocks(head_grad, y)
    home, table_part = call(
        merge_body,
        at,
        (keep, theirs, swap(away, "xl"), got),
        (jax.ShapeDtypeStruct(away.shape, BF), jax.ShapeDtypeStruct((strategies, wide), F32)),
        head_far,
    )

    wg_part = lax.psum_scatter(wg, "z", scatter_dimension=1, tiled=True)
    wg_other = swap(pick(wg_part, 1 - xh, 0), "xh")
    weight_sum = pick(wg_part, xh, 0).astype(F32) + wg_other.astype(F32)

    home = exchange(home.reshape(NY, half, wide), "y")
    table_part = table_part.reshape(NC, strategies // NC, wide)
    table_sum = pick(table_part, c, 0) + swap(pick(table_part, 1 - c, 0), "c")
    table_sum = table_sum + swap(table_sum, "xh")
    for bit in (1, 2, 4):
        sent = table_sum.astype(BF)
        far_sum = lax.ppermute(sent, "z", [(i, i ^ bit) for i in range(NZ)])
        if bit < 4:
            table_sum = sent.astype(F32) + far_sum.astype(F32)
        else:
            table_sum = call(add_body, at, (sent, far_sum), jax.ShapeDtypeStruct(sent.shape, F32), (home,))
    table_all = spread(table_sum, "y", NY).reshape(NC, 2, strategies // NC, wide)
    rest = jax.ShapeDtypeStruct(table_all.shape[1:], F32)
    rest = swap(call(take_body, (1 - c).reshape(1).astype(jnp.int32), (table_all,), rest, (wg_other,)), "c")
    table_sum = in_order(c, pick(table_all, c, 0), rest, 1)
    table_sum = table_sum.reshape(2, strategies, wide).transpose(1, 0, 2).reshape(strategies, cols)
    table_grad = jnp.dot(mixing.T, table_sum, precision=HIGHEST) * grad_scale

    parts = home.reshape(NC, 2, half, wide)
    back = swap(pick(parts, 1 - c, 0), "c")
    proj = in_order(c, pick(parts, c, 0), back, 1).reshape(2, rows, wide)
    gating = 1.0 + rows_of(members(ids, strategies), table)
    proj = jnp.concatenate([proj[0], proj[1]], axis=1).astype(F32)
    layer_out = (residual.reshape(rows, cols).astype(F32) + proj * gating).astype(BF)

    head_grad = scatter_y(head_grad, head_far, y, (home,)).astype(BF)

    shape = head_out.shape
    return layer_out.reshape(shape), head_grad.reshape(shape), weight_sum * grad_scale, table_grad


def solution(mesh):
    fine = Mesh(mesh.devices.reshape(XH, NY, NZ, XL, NC), ("xh", "y", "z", "xl", "c"))
    dp, mp = ("xh", "y", "z"), ("xl", "c")
    tokens = P(None, dp, mp)
    return jax.shard_map(
        on_device,
        mesh=fine,
        in_specs=(tokens, tokens, P(dp, mp), P(None, mp), P(), P(None, dp), tokens),
        out_specs=(tokens, tokens, P(dp, mp), P(None, mp)),
        check_vma=False,
    )
```

```python
import math

import jax
import jax.numpy as jnp
from jax import lax
from jax.experimental import pallas as pl
from jax.experimental.pallas import tpu as pltpu
from jax.sharding import Mesh, PartitionSpec as P

XH, NY, NZ, XL, NC = 2, 4, 8, 2, 2
BF = jnp.bfloat16
F32 = jnp.float32
HIGHEST = lax.Precision.HIGHEST


def swap(a, axis):
    return lax.ppermute(a, axis, [(0, 1), (1, 0)])


def exchange(a, axis):
    return lax.all_to_all(a, axis, 0, 0, tiled=True)


def spread(a, axis, n):
    return exchange(jnp.broadcast_to(a[None], (n,) + a.shape), axis)


def turn(a, k):
    return lax.ppermute(a, "y", [(i, (i + k) % NY) for i in range(NY)])


def gather_y(a, y):
    half = a.shape[1] // 2
    up, down = turn(a, 1), turn(a, -1)
    out = jnp.zeros((NY,) + a.shape, a.dtype)
    for piece, k in ((a, 0), (up, 1), (down, 3)):
        out = lax.dynamic_update_slice(out, piece[None], ((y - k) % NY, 0, 0))
    out = lax.dynamic_update_slice(out, turn(up[:, :half], 1)[None], ((y + 2) % NY, 0, 0))
    return lax.dynamic_update_slice(out, turn(down[:, half:], -1)[None], ((y + 2) % NY, 0, half))


def far_blocks(a, y):
    half = a.shape[2] // 2
    far = pick(a, (y + 2) % NY, 0)
    return turn(far[:, :half], 1), turn(far[:, half:], -1)


def scatter_y(a, far, y, after):
    block = jax.ShapeDtypeStruct(a.shape[1:], BF)
    up, down = call(pass_body, y.reshape(1).astype(jnp.int32), (a,) + far, (block, block), after)
    return pick(a, y, 0).astype(F32) + turn(up, 1).astype(F32) + turn(down, -1).astype(F32)


VMEM = pl.BlockSpec(memory_space=pltpu.VMEM)
SMEM = pl.BlockSpec(memory_space=pltpu.SMEM)
STEP = 256


def call(body, at, operands, out_shape, after=()):
    count = len(operands) + 1
    return pl.pallas_call(
        lambda *refs: body(*refs[:count], *refs[count + len(after) :]),
        out_shape=out_shape,
        in_specs=[SMEM] + [VMEM] * len(operands) + [pl.BlockSpec(memory_space=pl.ANY)] * len(after),
        out_specs=jax.tree.map(lambda _: VMEM, out_shape),
        compiler_params=pltpu.CompilerParams(vmem_limit_bytes=16 * 2**20),
        cost_estimate=pl.CostEstimate(flops=2**20, bytes_accessed=2**10, transcendentals=0),
    )(at, *operands, *after)


def pass_body(at, a, from_below, from_above, up, down):
    half = from_below.shape[1]
    above, below = lax.rem(at[0] + 1, NY), lax.rem(at[0] + NY - 1, NY)
    up[:, :half] = (a[above, :, :half].astype(F32) + from_below[...].astype(F32)).astype(BF)
    up[:, half:] = a[above, :, half:]
    down[:, :half] = a[below, :, :half]
    down[:, half:] = (a[below, :, half:].astype(F32) + from_above[...].astype(F32)).astype(BF)


def take_body(at, a, out):
    out[...] = a[at[0]]


def add_body(at, a, b, out):
    out[...] = a[...].astype(F32) + b[...].astype(F32)


def pair_body(at, own, other, out):
    out[at[0]] = own[...]
    out[1 - at[0]] = other[...]


def split3(a):
    parts = []
    for _ in range(3):
        parts.append(a.astype(BF))
        a = a - parts[-1].astype(F32)
    return parts


def hot_of(got, k, rows, strategies):
    ids = got[k, rows : rows + 16, :].astype(F32)[:1, :rows]
    return (lax.broadcasted_iota(jnp.int32, (strategies, rows), 0).astype(F32) == ids).astype(BF)


def table_body(at, mixing, own, there, out):
    where = pl.ds(pl.multiple_of(at[1] * out.shape[1], 128), out.shape[1])
    table = jnp.where(at[0] == 1, own[:, where].astype(F32), there[:, where].astype(F32))
    out[...] = jnp.dot(mixing[...], table, precision=HIGHEST, preferred_element_type=F32)


def gate_body(at, got, table, out):
    rows = out.shape[0] // NY
    parts = split3(table[...])
    for k in range(NY):
        hot = hot_of(got, k, rows, table.shape[0])
        gating = jnp.ones((rows, out.shape[1]), F32)
        for part in reversed(parts):
            gating += lax.dot_general(hot, part, (((0,), (0,)), ((), ())), preferred_element_type=F32)
        out[k * rows : (k + 1) * rows, :] = (got[k, :rows, :].astype(F32) * gating).astype(BF)


def home_body(at, stay, away, home):
    home[...] = (stay[...] + away[...].astype(F32)).astype(BF)


def keep_body(at, ho, w, theirs, near, far, away, stay, table):
    rows, half = ho[:, at[1]].reshape(-1, ho.shape[-1]), ho.shape[2]
    hot = [hot_of(near, k, half, table.shape[1]) for k in range(NY)]
    for which, x, cot in ((0, at[0], near), (1, 1 - at[0], far)):
        for n in range(0, w.shape[1], STEP):
            span = slice(n, n + STEP)
            chip = lax.dot_general(rows, w[x, span, :], (((1,), (1,)), ((), ())), preferred_element_type=F32)
            chip = chip.astype(BF).astype(F32) + theirs[x, :, span].astype(F32)
            if which:
                away[:, span] = chip.astype(BF)
            else:
                stay[:, span] = chip
            total = jnp.zeros((table.shape[1], STEP), F32)
            for k in range(NY):
                for part in split3(cot[k, :half, span].astype(F32) * chip[k * half : (k + 1) * half]):
                    total += jnp.dot(hot[k], part, preferred_element_type=F32)
            table[which, :, span] = total


def project_body(at, ho, w, out):
    rows = ho[:, at[0]].reshape(-1, ho.shape[-1])
    for x in range(XL):
        for n in range(0, w.shape[1], STEP):
            out[x, :, n : n + STEP] = lax.dot_general(
                rows, w[x, n : n + STEP, :], (((1,), (1,)), ((), ())), preferred_element_type=F32
            ).astype(BF)


def weight_body(at, near, far, near_c, far_c, ho, out):
    xl, c = at[0], at[1]
    mine = ho[:, c].reshape(-1, ho.shape[-1])
    theirs = ho[:, 1 - c].reshape(-1, ho.shape[-1])
    over = (((0,), (0,)), ((), ()))
    for x, p, q in ((xl, near, near_c), (1 - xl, far, far_c)):
        for n in range(0, out.shape[-1], STEP):
            total = lax.dot_general(p[...], mine[:, n : n + STEP], over, preferred_element_type=F32)
            total += lax.dot_general(q[...], theirs[:, n : n + STEP], over, preferred_element_type=F32)
            out[x, :, n : n + STEP] = total.astype(BF)


def head_body(at, near, far, near_c, far_c, w, out):
    xl, c = at[0], at[1]
    for half, p, q in ((c, near, far), (1 - c, near_c, far_c)):
        for n in range(0, out.shape[-1], STEP):
            total = jnp.dot(p[...], w[xl, :, n : n + STEP], preferred_element_type=F32)
            total += jnp.dot(q[...], w[1 - xl, :, n : n + STEP], preferred_element_type=F32)
            out[:, half, :, n : n + STEP] = total.astype(BF).reshape(NY, -1, STEP)


def pick(a, at, dim):
    return lax.dynamic_index_in_dim(a, at, dim, keepdims=False)


def in_order(index, own, other, dim):
    first = jnp.where(index == 0, own, other)
    second = jnp.where(index == 0, other, own)
    return jnp.stack([first, second], axis=dim)


def mixture(meta_graph):
    counts = meta_graph.astype(F32)
    totals = jnp.maximum(jnp.sum(counts, axis=1, keepdims=True), 1.0)
    return jnp.eye(meta_graph.shape[0], dtype=F32) + counts / totals


def members(ids, strategies):
    return (lax.broadcasted_iota(jnp.int32, (strategies, 1), 0) == ids[None, :]).astype(F32)


def rows_of(one_hot, table):
    return lax.dot_general(one_hot, table, (((0,), (0,)), ((), ())), precision=HIGHEST, preferred_element_type=F32)


def on_device(head_out, residual, out_weight, strategy_table, meta_graph, strategy_ids, cotangent):
    batches, local_rows, cols = head_out.shape
    rows, half, wide = batches * local_rows, batches * local_rows // 2, cols // 2
    strategies = meta_graph.shape[0]
    wr = out_weight.shape[0]
    pad = 16
    xh, y, xl, c = (lax.axis_index(name) for name in ("xh", "y", "xl", "c"))
    grad_scale = 1.0 / math.sqrt(rows * XH * NY * NZ)

    ho = head_out.reshape(rows, cols)
    cot = cotangent.reshape(rows, cols)
    ids = strategy_ids.reshape(rows)

    cot_parts = cot.reshape(NC, half, cols)
    other = swap(pick(cot_parts, 1 - c, 0), "c")
    mine = in_order(c, pick(cot_parts, c, 0), other, 0)
    by_y = mine.reshape(NC, half, 2, wide).transpose(0, 2, 1, 3).reshape(NY, half, wide)
    tag = pick(ids.reshape(NC, half), c, 0).astype(BF)
    tag = jnp.broadcast_to(jnp.pad(tag, (0, wide - half))[None, None], (NY, pad, wide))
    got = exchange(jnp.concatenate([by_y, tag], axis=1), "y")

    ho_y = gather_y(ho, y).reshape(NY, NC, half, cols)

    unit = call(
        pair_body,
        xh.reshape(1).astype(jnp.int32),
        (out_weight, swap(out_weight, "xh")),
        jax.ShapeDtypeStruct((XH,) + out_weight.shape, BF),
        (other,),
    )
    weight = lax.all_gather(unit, "z", axis=1, tiled=True)

    mixing = mixture(meta_graph)
    table = jnp.dot(mixing, strategy_table.astype(F32), precision=HIGHEST)
    there = swap(strategy_table, "c")
    source = jnp.stack([(y // 2 == c).astype(jnp.int32), (y % 2).astype(jnp.int32)])
    table_y = call(table_body, source, (mixing, strategy_table, there), jax.ShapeDtypeStruct((strategies, wide), F32))
    gate = lambda block, table: call(gate_body, source, (block, table), jax.ShapeDtypeStruct((NY * half, wide), BF))
    got_far = swap(got, "xl")

    near, far = gate(got, table_y), gate(got_far, swap(table_y, "xl"))
    pieces = (near, far, swap(near, "c"), swap(far, "c"))
    at = jnp.stack([xl, c]).astype(jnp.int32)

    give = call(
        project_body,
        (1 - c).reshape(1).astype(jnp.int32),
        (ho_y, weight),
        jax.ShapeDtypeStruct((XL, NY * half, wide), BF),
        (far,),
    )
    theirs = swap(give, "c")
    wg = call(weight_body, at, pieces + (ho_y,), jax.ShapeDtypeStruct((XH, NZ * wr, cols), BF), (give,))
    away, stay, table_part = call(
        keep_body,
        at,
        (ho_y, weight, theirs, got, got_far),
        (
            jax.ShapeDtypeStruct((NY * half, wide), BF),
            jax.ShapeDtypeStruct((NY * half, wide), F32),
            jax.ShapeDtypeStruct((XL, strategies, wide), F32),
        ),
        (wg,),
    )
    head_grad = call(head_body, at, pieces + (weight,), jax.ShapeDtypeStruct((NY, NC, half, cols), BF), (away,))
    head_grad = head_grad.reshape(NY, rows, cols)
    head_far = far_blocks(head_grad, y)
    wg_part = lax.psum_scatter(wg, "z", scatter_dimension=1, tiled=True)
    wg_other = swap(pick(wg_part, 1 - xh, 0), "xh")
    weight_sum = pick(wg_part, xh, 0).astype(F32) + wg_other.astype(F32)

    table_part = table_part.reshape(XL, NC, strategies // NC, wide)
    table_sum = pick(table_part, c, 1) + swap(pick(table_part, 1 - c, 1), "c")
    table_sum = table_sum[0] + swap(table_sum[1], "xl")
    table_sum = table_sum + swap(table_sum, "xh")
    beside = lambda a, bit: lax.ppermute(a, "z", [(i, i ^ bit) for i in range(NZ)])
    sent = table_sum.astype(BF)
    sent = (sent.astype(F32) + beside(sent, 1).astype(F32)).astype(BF)
    home = jax.ShapeDtypeStruct(away.shape, BF)
    home = call(home_body, at, (stay, swap(away, "xl")), home, head_far + (sent,))
    home = exchange(home.reshape(NY, half, wide), "y")
    sent = (sent.astype(F32) + beside(sent, 2).astype(F32)).astype(BF)
    table_sum = call(add_body, at, (sent, beside(sent, 4)), jax.ShapeDtypeStruct(sent.shape, F32), (home,))
    table_all = spread(table_sum, "y", NY).reshape(NC, 2, strategies // NC, wide)
    rest = jax.ShapeDtypeStruct(table_all.shape[1:], F32)
    rest = swap(call(take_body, (1 - c).reshape(1).astype(jnp.int32), (table_all,), rest, (wg_other,)), "c")
    table_sum = in_order(c, pick(table_all, c, 0), rest, 1)
    table_sum = table_sum.reshape(2, strategies, wide).transpose(1, 0, 2).reshape(strategies, cols)
    table_grad = jnp.dot(mixing.T, table_sum, precision=HIGHEST) * grad_scale

    parts = home.reshape(NC, 2, half, wide)
    back = swap(pick(parts, 1 - c, 0), "c")
    proj = in_order(c, pick(parts, c, 0), back, 1).reshape(2, rows, wide)
    gating = 1.0 + rows_of(members(ids, strategies), table)
    proj = jnp.concatenate([proj[0], proj[1]], axis=1).astype(F32)
    layer_out = (residual.reshape(rows, cols).astype(F32) + proj * gating).astype(BF)

    head_grad = scatter_y(head_grad, head_far, y, (home,)).astype(BF)

    shape = head_out.shape
    return layer_out.reshape(shape), head_grad.reshape(shape), weight_sum * grad_scale, table_grad


def solution(mesh):
    fine = Mesh(mesh.devices.reshape(XH, NY, NZ, XL, NC), ("xh", "y", "z", "xl", "c"))
    dp, mp = ("xh", "y", "z"), ("xl", "c")
    tokens = P(None, dp, mp)
    return jax.shard_map(
        on_device,
        mesh=fine,
        in_specs=(tokens, tokens, P(dp, mp), P(None, mp), P(), P(None, dp), tokens),
        out_specs=(tokens, tokens, P(dp, mp), P(None, mp)),
        check_vma=False,
    )
```

```python
import math

import jax
import jax.numpy as jnp
from jax import lax
from jax.experimental import pallas as pl
from jax.experimental.pallas import tpu as pltpu
from jax.sharding import Mesh, PartitionSpec as P

XH, NY, NZ, XL, NC = 2, 4, 8, 2, 2
BF = jnp.bfloat16
F32 = jnp.float32
HIGHEST = lax.Precision.HIGHEST


def swap(a, axis):
    return lax.ppermute(a, axis, [(0, 1), (1, 0)])


def exchange(a, axis):
    return lax.all_to_all(a, axis, 0, 0, tiled=True)


def spread(a, axis, n):
    return exchange(jnp.broadcast_to(a[None], (n,) + a.shape), axis)


def turn(a, k):
    return lax.ppermute(a, "y", [(i, (i + k) % NY) for i in range(NY)])


def gather_y(a, y):
    half = a.shape[1] // 2
    up, down = turn(a, 1), turn(a, -1)
    out = jnp.zeros((NY,) + a.shape, a.dtype)
    for piece, k in ((a, 0), (up, 1), (down, 3)):
        out = lax.dynamic_update_slice(out, piece[None], ((y - k) % NY, 0, 0))
    out = lax.dynamic_update_slice(out, turn(up[:, :half], 1)[None], ((y + 2) % NY, 0, 0))
    return lax.dynamic_update_slice(out, turn(down[:, half:], -1)[None], ((y + 2) % NY, 0, half))


def far_blocks(a, y):
    half = a.shape[2] // 2
    far = pick(a, (y + 2) % NY, 0)
    return turn(far[:, :half], 1), turn(far[:, half:], -1)


def near_blocks(a, far, y, after):
    block = jax.ShapeDtypeStruct(a.shape[1:], BF)
    up, down = call(pass_body, y.reshape(1).astype(jnp.int32), (a,) + far, (block, block), after)
    return turn(up, 1), turn(down, -1)


VMEM = pl.BlockSpec(memory_space=pltpu.VMEM)
SMEM = pl.BlockSpec(memory_space=pltpu.SMEM)
STEP = 256


def call(body, at, operands, out_shape, after=()):
    count = len(operands) + 1
    return pl.pallas_call(
        lambda *refs: body(*refs[:count], *refs[count + len(after) :]),
        out_shape=out_shape,
        in_specs=[SMEM] + [VMEM] * len(operands) + [pl.BlockSpec(memory_space=pl.ANY)] * len(after),
        out_specs=jax.tree.map(lambda _: VMEM, out_shape),
        compiler_params=pltpu.CompilerParams(vmem_limit_bytes=16 * 2**20),
        cost_estimate=pl.CostEstimate(flops=2**20, bytes_accessed=2**10, transcendentals=0),
    )(at, *operands, *after)


def pass_body(at, a, from_below, from_above, up, down):
    half = from_below.shape[1]
    above, below = lax.rem(at[0] + 1, NY), lax.rem(at[0] + NY - 1, NY)
    up[:, :half] = (a[above, :, :half].astype(F32) + from_below[...].astype(F32)).astype(BF)
    up[:, half:] = a[above, :, half:]
    down[:, :half] = a[below, :, :half]
    down[:, half:] = (a[below, :, half:].astype(F32) + from_above[...].astype(F32)).astype(BF)


def take_body(at, a, out):
    out[...] = a[at[0]]


def add_body(at, a, b, out):
    out[...] = a[...].astype(F32) + b[...].astype(F32)


def pair_body(at, own, other, out):
    out[at[0]] = own[...]
    out[1 - at[0]] = other[...]


def split3(a):
    parts = []
    for _ in range(3):
        parts.append(a.astype(BF))
        a = a - parts[-1].astype(F32)
    return parts


def hot_of(got, k, rows, strategies):
    ids = got[k, rows : rows + 16, :].astype(F32)[:1, :rows]
    return (lax.broadcasted_iota(jnp.int32, (strategies, rows), 0).astype(F32) == ids).astype(BF)


def table_body(at, mixing, own, there, out):
    where = pl.ds(pl.multiple_of(at[1] * out.shape[1], 128), out.shape[1])
    table = jnp.where(at[0] == 1, own[:, where].astype(F32), there[:, where].astype(F32))
    out[...] = jnp.dot(mixing[...], table, precision=HIGHEST, preferred_element_type=F32)


def gate_body(at, got, table, out):
    rows = out.shape[0] // NY
    parts = split3(table[...])
    for k in range(NY):
        hot = hot_of(got, k, rows, table.shape[0])
        gating = jnp.ones((rows, out.shape[1]), F32)
        for part in reversed(parts):
            gating += lax.dot_general(hot, part, (((0,), (0,)), ((), ())), preferred_element_type=F32)
        out[k * rows : (k + 1) * rows, :] = (got[k, :rows, :].astype(F32) * gating).astype(BF)


def home_body(at, stay, away, home):
    home[...] = (stay[...] + away[...].astype(F32)).astype(BF)


def keep_body(at, ho, w, theirs, near, far, away, stay, table):
    rows, half = ho[:, at[1]].reshape(-1, ho.shape[-1]), ho.shape[2]
    hot = [hot_of(near, k, half, table.shape[1]) for k in range(NY)]
    for which, x, cot in ((0, at[0], near), (1, 1 - at[0], far)):
        for n in range(0, w.shape[1], STEP):
            span = slice(n, n + STEP)
            chip = lax.dot_general(rows, w[x, span, :], (((1,), (1,)), ((), ())), preferred_element_type=F32)
            chip = chip.astype(BF).astype(F32) + theirs[x, :, span].astype(F32)
            if which:
                away[:, span] = chip.astype(BF)
            else:
                stay[:, span] = chip
            total = jnp.zeros((table.shape[1], STEP), F32)
            for k in range(NY):
                for part in split3(cot[k, :half, span].astype(F32) * chip[k * half : (k + 1) * half]):
                    total += jnp.dot(hot[k], part, preferred_element_type=F32)
            table[which, :, span] = total


def project_body(at, ho, w, out):
    rows = ho[:, at[0]].reshape(-1, ho.shape[-1])
    for x in range(XL):
        for n in range(0, w.shape[1], STEP):
            out[x, :, n : n + STEP] = lax.dot_general(
                rows, w[x, n : n + STEP, :], (((1,), (1,)), ((), ())), preferred_element_type=F32
            ).astype(BF)


def weight_body(at, near, far, near_c, far_c, ho, out):
    xl, c = at[0], at[1]
    mine = ho[:, c].reshape(-1, ho.shape[-1])
    theirs = ho[:, 1 - c].reshape(-1, ho.shape[-1])
    over = (((0,), (0,)), ((), ()))
    for x, p, q in ((xl, near, near_c), (1 - xl, far, far_c)):
        for n in range(0, out.shape[-1], STEP):
            total = lax.dot_general(p[...], mine[:, n : n + STEP], over, preferred_element_type=F32)
            total += lax.dot_general(q[...], theirs[:, n : n + STEP], over, preferred_element_type=F32)
            out[x, :, n : n + STEP] = total.astype(BF)


def head_body(at, near, far, near_c, far_c, w, out):
    xl, c = at[0], at[1]
    for half, p, q in ((c, near, far), (1 - c, near_c, far_c)):
        for n in range(0, out.shape[-1], STEP):
            total = jnp.dot(p[...], w[xl, :, n : n + STEP], preferred_element_type=F32)
            total += jnp.dot(q[...], w[1 - xl, :, n : n + STEP], preferred_element_type=F32)
            out[:, half, :, n : n + STEP] = total.astype(BF).reshape(NY, -1, STEP)


def pick(a, at, dim):
    return lax.dynamic_index_in_dim(a, at, dim, keepdims=False)


def in_order(index, own, other, dim):
    first = jnp.where(index == 0, own, other)
    second = jnp.where(index == 0, other, own)
    return jnp.stack([first, second], axis=dim)


def mixture(meta_graph):
    counts = meta_graph.astype(F32)
    totals = jnp.maximum(jnp.sum(counts, axis=1, keepdims=True), 1.0)
    return jnp.eye(meta_graph.shape[0], dtype=F32) + counts / totals


def members(ids, strategies):
    return (lax.broadcasted_iota(jnp.int32, (strategies, 1), 0) == ids[None, :]).astype(F32)


def rows_of(one_hot, table):
    return lax.dot_general(one_hot, table, (((0,), (0,)), ((), ())), precision=HIGHEST, preferred_element_type=F32)


def on_device(head_out, residual, out_weight, strategy_table, meta_graph, strategy_ids, cotangent):
    batches, local_rows, cols = head_out.shape
    rows, half, wide = batches * local_rows, batches * local_rows // 2, cols // 2
    strategies = meta_graph.shape[0]
    wr = out_weight.shape[0]
    pad = 16
    xh, y, xl, c = (lax.axis_index(name) for name in ("xh", "y", "xl", "c"))
    grad_scale = 1.0 / math.sqrt(rows * XH * NY * NZ)

    ho = head_out.reshape(rows, cols)
    cot = cotangent.reshape(rows, cols)
    ids = strategy_ids.reshape(rows)

    cot_parts = cot.reshape(NC, half, cols)
    other = swap(pick(cot_parts, 1 - c, 0), "c")
    mine = in_order(c, pick(cot_parts, c, 0), other, 0)
    by_y = mine.reshape(NC, half, 2, wide).transpose(0, 2, 1, 3).reshape(NY, half, wide)
    tag = pick(ids.reshape(NC, half), c, 0).astype(BF)
    tag = jnp.broadcast_to(jnp.pad(tag, (0, wide - half))[None, None], (NY, pad, wide))
    got = exchange(jnp.concatenate([by_y, tag], axis=1), "y")

    ho_y = gather_y(ho, y).reshape(NY, NC, half, cols)

    unit = call(
        pair_body,
        xh.reshape(1).astype(jnp.int32),
        (out_weight, swap(out_weight, "xh")),
        jax.ShapeDtypeStruct((XH,) + out_weight.shape, BF),
        (other,),
    )
    weight = lax.all_gather(unit, "z", axis=1, tiled=True)

    mixing = mixture(meta_graph)
    table = jnp.dot(mixing, strategy_table.astype(F32), precision=HIGHEST)
    there = swap(strategy_table, "c")
    source = jnp.stack([(y // 2 == c).astype(jnp.int32), (y % 2).astype(jnp.int32)])
    table_y = call(table_body, source, (mixing, strategy_table, there), jax.ShapeDtypeStruct((strategies, wide), F32))
    gate = lambda block, table: call(gate_body, source, (block, table), jax.ShapeDtypeStruct((NY * half, wide), BF))
    got_far = swap(got, "xl")

    near, far = gate(got, table_y), gate(got_far, swap(table_y, "xl"))
    pieces = (near, far, swap(near, "c"), swap(far, "c"))
    at = jnp.stack([xl, c]).astype(jnp.int32)

    give = call(
        project_body,
        (1 - c).reshape(1).astype(jnp.int32),
        (ho_y, weight),
        jax.ShapeDtypeStruct((XL, NY * half, wide), BF),
        (far, near),
    )
    theirs = swap(give, "c")
    wg = call(weight_body, at, pieces + (ho_y,), jax.ShapeDtypeStruct((XH, NZ * wr, cols), BF), (give,))
    head_grad = call(head_body, at, pieces + (weight,), jax.ShapeDtypeStruct((NY, NC, half, cols), BF), (wg,))
    head_grad = head_grad.reshape(NY, rows, cols)
    head_far = far_blocks(head_grad, y)
    away, stay, table_part = call(
        keep_body,
        at,
        (ho_y, weight, theirs, got, got_far),
        (
            jax.ShapeDtypeStruct((NY * half, wide), BF),
            jax.ShapeDtypeStruct((NY * half, wide), F32),
            jax.ShapeDtypeStruct((XL, strategies, wide), F32),
        ),
        (head_grad,),
    )

    wg_part = lax.psum_scatter(wg, "z", scatter_dimension=1, tiled=True)
    wg_other = swap(pick(wg_part, 1 - xh, 0), "xh")
    weight_sum = pick(wg_part, xh, 0).astype(F32) + wg_other.astype(F32)

    table_part = table_part.reshape(XL, NC, strategies // NC, wide)
    sent = (pick(table_part, c, 1) + swap(pick(table_part, 1 - c, 1), "c")).astype(BF)
    head_near = near_blocks(head_grad, head_far, y, (sent,))
    for bit in (1, 2, 4):
        if bit == 4:
            home = jax.ShapeDtypeStruct(away.shape, BF)
            home = call(home_body, at, (stay, swap(away, "xl")), home, head_near + (sent,))
            home = exchange(home.reshape(NY, half, wide), "y")
        table_sum = sent.astype(F32) + lax.ppermute(sent, "z", [(i, i ^ bit) for i in range(NZ)]).astype(F32)
        sent = table_sum.astype(BF)
    table_sum = table_sum[0] + swap(table_sum[1], "xl")
    table_sum = call(
        add_body, at, (table_sum, swap(table_sum, "xh")), jax.ShapeDtypeStruct(table_sum.shape, F32), (home,)
    )
    table_all = spread(table_sum, "y", NY).reshape(NC, 2, strategies // NC, wide)
    rest = jax.ShapeDtypeStruct(table_all.shape[1:], F32)
    rest = swap(call(take_body, (1 - c).reshape(1).astype(jnp.int32), (table_all,), rest, (wg_other,)), "c")
    table_sum = in_order(c, pick(table_all, c, 0), rest, 1)
    table_sum = table_sum.reshape(2, strategies, wide).transpose(1, 0, 2).reshape(strategies, cols)
    table_grad = jnp.dot(mixing.T, table_sum, precision=HIGHEST) * grad_scale

    parts = home.reshape(NC, 2, half, wide)
    back = swap(pick(parts, 1 - c, 0), "c")
    proj = in_order(c, pick(parts, c, 0), back, 1).reshape(2, rows, wide)
    gating = 1.0 + rows_of(members(ids, strategies), table)
    proj = jnp.concatenate([proj[0], proj[1]], axis=1).astype(F32)
    layer_out = (residual.reshape(rows, cols).astype(F32) + proj * gating).astype(BF)

    head_grad = pick(head_grad, y, 0).astype(F32) + head_near[0].astype(F32) + head_near[1].astype(F32)

    shape = head_out.shape
    return layer_out.reshape(shape), head_grad.astype(BF).reshape(shape), weight_sum * grad_scale, table_grad


def solution(mesh):
    fine = Mesh(mesh.devices.reshape(XH, NY, NZ, XL, NC), ("xh", "y", "z", "xl", "c"))
    dp, mp = ("xh", "y", "z"), ("xl", "c")
    tokens = P(None, dp, mp)
    return jax.shard_map(
        on_device,
        mesh=fine,
        in_specs=(tokens, tokens, P(dp, mp), P(None, mp), P(), P(None, dp), tokens),
        out_specs=(tokens, tokens, P(dp, mp), P(None, mp)),
        check_vma=False,
    )
```

```python
import math

import jax
import jax.numpy as jnp
from jax import lax
from jax.experimental import pallas as pl
from jax.experimental.pallas import tpu as pltpu
from jax.sharding import Mesh, PartitionSpec as P

XH, NY, NZ, XL, NC = 2, 4, 8, 2, 2
BF = jnp.bfloat16
F32 = jnp.float32
HIGHEST = lax.Precision.HIGHEST


def swap(a, axis):
    return lax.ppermute(a, axis, [(0, 1), (1, 0)])


def exchange(a, axis):
    return lax.all_to_all(a, axis, 0, 0, tiled=True)


def spread(a, axis, n):
    return exchange(jnp.broadcast_to(a[None], (n,) + a.shape), axis)


def turn(a, k):
    return lax.ppermute(a, "y", [(i, (i + k) % NY) for i in range(NY)])


def gather_y(a, y):
    half = a.shape[1] // 2
    up, down = turn(a, 1), turn(a, -1)
    out = jnp.zeros((NY,) + a.shape, a.dtype)
    for piece, k in ((a, 0), (up, 1), (down, 3)):
        out = lax.dynamic_update_slice(out, piece[None], ((y - k) % NY, 0, 0))
    out = lax.dynamic_update_slice(out, turn(up[:, :half], 1)[None], ((y + 2) % NY, 0, 0))
    return lax.dynamic_update_slice(out, turn(down[:, half:], -1)[None], ((y + 2) % NY, 0, half))


def far_blocks(a, y):
    half = a.shape[2] // 2
    far = pick(a, (y + 2) % NY, 0)
    return turn(far[:, :half], 1), turn(far[:, half:], -1)


def near_blocks(a, far, y, after):
    block = jax.ShapeDtypeStruct(a.shape[1:], BF)
    up, down = call(pass_body, y.reshape(1).astype(jnp.int32), (a,) + far, (block, block), after)
    return turn(up, 1), turn(down, -1)


VMEM = pl.BlockSpec(memory_space=pltpu.VMEM)
SMEM = pl.BlockSpec(memory_space=pltpu.SMEM)
STEP = 256


def call(body, at, operands, out_shape, after=()):
    count = len(operands) + 1
    return pl.pallas_call(
        lambda *refs: body(*refs[:count], *refs[count + len(after) :]),
        out_shape=out_shape,
        in_specs=[SMEM] + [VMEM] * len(operands) + [pl.BlockSpec(memory_space=pl.ANY)] * len(after),
        out_specs=jax.tree.map(lambda _: VMEM, out_shape),
        compiler_params=pltpu.CompilerParams(vmem_limit_bytes=16 * 2**20),
        cost_estimate=pl.CostEstimate(flops=2**20, bytes_accessed=2**10, transcendentals=0),
    )(at, *operands, *after)


def pass_body(at, a, from_below, from_above, up, down):
    half = from_below.shape[1]
    above, below = lax.rem(at[0] + 1, NY), lax.rem(at[0] + NY - 1, NY)
    up[:, :half] = (a[above, :, :half].astype(F32) + from_below[...].astype(F32)).astype(BF)
    up[:, half:] = a[above, :, half:]
    down[:, :half] = a[below, :, :half]
    down[:, half:] = (a[below, :, half:].astype(F32) + from_above[...].astype(F32)).astype(BF)


def take_body(at, a, out):
    out[...] = a[at[0]]


def add_body(at, a, b, out):
    out[...] = (a[...].astype(F32) + b[...].astype(F32)).astype(out.dtype)


def pair_body(at, own, other, out):
    out[at[0]] = own[...]
    out[1 - at[0]] = other[...]


def split3(a):
    parts = []
    for _ in range(3):
        parts.append(a.astype(BF))
        a = a - parts[-1].astype(F32)
    return parts


def hot_of(got, k, rows, strategies):
    ids = got[k, rows : rows + 16, :].astype(F32)[:1, :rows]
    return (lax.broadcasted_iota(jnp.int32, (strategies, rows), 0).astype(F32) == ids).astype(BF)


def table_body(at, mixing, own, there, out):
    where = pl.ds(pl.multiple_of(at[1] * out.shape[1], 128), out.shape[1])
    table = jnp.where(at[0] == 1, own[:, where].astype(F32), there[:, where].astype(F32))
    out[...] = jnp.dot(mixing[...], table, precision=HIGHEST, preferred_element_type=F32)


def gate_body(at, got, table, out):
    rows = out.shape[0] // NY
    parts = split3(table[...])
    for k in range(NY):
        hot = hot_of(got, k, rows, table.shape[0])
        gating = jnp.ones((rows, out.shape[1]), F32)
        for part in reversed(parts):
            gating += lax.dot_general(hot, part, (((0,), (0,)), ((), ())), preferred_element_type=F32)
        out[k * rows : (k + 1) * rows, :] = (got[k, :rows, :].astype(F32) * gating).astype(BF)


def home_body(at, stay, away, home):
    home[...] = (stay[...] + away[...].astype(F32)).astype(BF)


def keep_body(at, ho, w, theirs, near, far, away, stay, table):
    rows, half = ho[:, at[1]].reshape(-1, ho.shape[-1]), ho.shape[2]
    hot = [hot_of(near, k, half, table.shape[1]) for k in range(NY)]
    for which, x, cot in ((0, at[0], near), (1, 1 - at[0], far)):
        for n in range(0, w.shape[1], STEP):
            span = slice(n, n + STEP)
            chip = lax.dot_general(rows, w[x, span, :], (((1,), (1,)), ((), ())), preferred_element_type=F32)
            chip = chip.astype(BF).astype(F32) + theirs[x, :, span].astype(F32)
            if which:
                away[:, span] = chip.astype(BF)
            else:
                stay[:, span] = chip
            total = jnp.zeros((table.shape[1], STEP), F32)
            for k in range(NY):
                for part in split3(cot[k, :half, span].astype(F32) * chip[k * half : (k + 1) * half]):
                    total += jnp.dot(hot[k], part, preferred_element_type=F32)
            table[which, :, span] = total


def project_body(at, ho, w, out):
    rows = ho[:, at[0]].reshape(-1, ho.shape[-1])
    for x in range(XL):
        for n in range(0, w.shape[1], STEP):
            out[x, :, n : n + STEP] = lax.dot_general(
                rows, w[x, n : n + STEP, :], (((1,), (1,)), ((), ())), preferred_element_type=F32
            ).astype(BF)


def weight_body(at, near, far, near_c, far_c, ho, out):
    xl, c = at[0], at[1]
    mine = ho[:, c].reshape(-1, ho.shape[-1])
    theirs = ho[:, 1 - c].reshape(-1, ho.shape[-1])
    over = (((0,), (0,)), ((), ()))
    for x, p, q in ((xl, near, near_c), (1 - xl, far, far_c)):
        for n in range(0, out.shape[-1], STEP):
            total = lax.dot_general(p[...], mine[:, n : n + STEP], over, preferred_element_type=F32)
            total += lax.dot_general(q[...], theirs[:, n : n + STEP], over, preferred_element_type=F32)
            out[x, :, n : n + STEP] = total.astype(BF)


def head_body(at, near, far, near_c, far_c, w, out):
    xl, c = at[0], at[1]
    for half, p, q in ((c, near, far), (1 - c, near_c, far_c)):
        for n in range(0, out.shape[-1], STEP):
            total = jnp.dot(p[...], w[xl, :, n : n + STEP], preferred_element_type=F32)
            total += jnp.dot(q[...], w[1 - xl, :, n : n + STEP], preferred_element_type=F32)
            out[:, half, :, n : n + STEP] = total.astype(BF).reshape(NY, -1, STEP)


def pick(a, at, dim):
    return lax.dynamic_index_in_dim(a, at, dim, keepdims=False)


def in_order(index, own, other, dim):
    first = jnp.where(index == 0, own, other)
    second = jnp.where(index == 0, other, own)
    return jnp.stack([first, second], axis=dim)


def mixture(meta_graph):
    counts = meta_graph.astype(F32)
    totals = jnp.maximum(jnp.sum(counts, axis=1, keepdims=True), 1.0)
    return jnp.eye(meta_graph.shape[0], dtype=F32) + counts / totals


def members(ids, strategies):
    return (lax.broadcasted_iota(jnp.int32, (strategies, 1), 0) == ids[None, :]).astype(F32)


def rows_of(one_hot, table):
    return lax.dot_general(one_hot, table, (((0,), (0,)), ((), ())), precision=HIGHEST, preferred_element_type=F32)


def on_device(head_out, residual, out_weight, strategy_table, meta_graph, strategy_ids, cotangent):
    batches, local_rows, cols = head_out.shape
    rows, half, wide = batches * local_rows, batches * local_rows // 2, cols // 2
    strategies = meta_graph.shape[0]
    wr = out_weight.shape[0]
    pad = 16
    xh, y, xl, c = (lax.axis_index(name) for name in ("xh", "y", "xl", "c"))
    grad_scale = 1.0 / math.sqrt(rows * XH * NY * NZ)

    ho = head_out.reshape(rows, cols)
    cot = cotangent.reshape(rows, cols)
    ids = strategy_ids.reshape(rows)

    cot_parts = cot.reshape(NC, half, cols)
    other = swap(pick(cot_parts, 1 - c, 0), "c")
    mine = in_order(c, pick(cot_parts, c, 0), other, 0)
    by_y = mine.reshape(NC, half, 2, wide).transpose(0, 2, 1, 3).reshape(NY, half, wide)
    tag = pick(ids.reshape(NC, half), c, 0).astype(BF)
    tag = jnp.broadcast_to(jnp.pad(tag, (0, wide - half))[None, None], (NY, pad, wide))
    got = exchange(jnp.concatenate([by_y, tag], axis=1), "y")

    ho_y = gather_y(ho, y).reshape(NY, NC, half, cols)

    unit = call(
        pair_body,
        xh.reshape(1).astype(jnp.int32),
        (out_weight, swap(out_weight, "xh")),
        jax.ShapeDtypeStruct((XH,) + out_weight.shape, BF),
        (other,),
    )
    weight = lax.all_gather(unit, "z", axis=1, tiled=True)

    mixing = mixture(meta_graph)
    table = jnp.dot(mixing, strategy_table.astype(F32), precision=HIGHEST)
    there = swap(strategy_table, "c")
    source = jnp.stack([(y // 2 == c).astype(jnp.int32), (y % 2).astype(jnp.int32)])
    table_y = call(table_body, source, (mixing, strategy_table, there), jax.ShapeDtypeStruct((strategies, wide), F32))
    gate = lambda block, table: call(gate_body, source, (block, table), jax.ShapeDtypeStruct((NY * half, wide), BF))
    got_far = swap(got, "xl")

    near, far = gate(got, table_y), gate(got_far, swap(table_y, "xl"))
    pieces = (near, far, swap(near, "c"), swap(far, "c"))
    at = jnp.stack([xl, c]).astype(jnp.int32)

    give = call(
        project_body,
        (1 - c).reshape(1).astype(jnp.int32),
        (ho_y, weight),
        jax.ShapeDtypeStruct((XL, NY * half, wide), BF),
        (far, near),
    )
    theirs = swap(give, "c")
    wg = call(weight_body, at, pieces + (ho_y,), jax.ShapeDtypeStruct((XH, NZ * wr, cols), BF), (give,))
    head_grad = call(head_body, at, pieces + (weight,), jax.ShapeDtypeStruct((NY, NC, half, cols), BF), (wg,))
    head_grad = head_grad.reshape(NY, rows, cols)
    head_far = far_blocks(head_grad, y)
    away, stay, table_part = call(
        keep_body,
        at,
        (ho_y, weight, theirs, got, got_far),
        (
            jax.ShapeDtypeStruct((NY * half, wide), BF),
            jax.ShapeDtypeStruct((NY * half, wide), F32),
            jax.ShapeDtypeStruct((XL, strategies, wide), F32),
        ),
        (head_grad,),
    )

    wg_part = lax.psum_scatter(wg, "z", scatter_dimension=1, tiled=True)
    wg_other = swap(pick(wg_part, 1 - xh, 0), "xh")
    weight_sum = pick(wg_part, xh, 0).astype(F32) + wg_other.astype(F32)

    table_part = table_part.reshape(XL, NC, strategies // NC, wide)
    sent = (pick(table_part, c, 1) + swap(pick(table_part, 1 - c, 1), "c")).astype(BF)
    head_near = near_blocks(head_grad, head_far, y, (sent,))
    beside = lambda a, bit: lax.ppermute(a, "z", [(i, i ^ bit) for i in range(NZ)])
    sent = (sent.astype(F32) + beside(sent, 1).astype(F32)).astype(BF)
    sent = (sent.astype(F32) + beside(sent, 2).astype(F32)).astype(BF)
    home = jax.ShapeDtypeStruct(away.shape, BF)
    home = call(home_body, at, (stay, swap(away, "xl")), home, head_near + (sent,))
    table_sum = call(add_body, at, (sent, beside(sent, 4)), jax.ShapeDtypeStruct(sent.shape, F32), (home,))
    home = exchange(home.reshape(NY, half, wide), "y")
    table_sum = table_sum[0] + swap(table_sum[1], "xl")
    table_sum = call(
        add_body, at, (table_sum, swap(table_sum, "xh")), jax.ShapeDtypeStruct(table_sum.shape, F32), (home, wg_other)
    )
    table_all = spread(table_sum, "y", NY).reshape(NC, 2, strategies // NC, wide)
    rest = swap(pick(table_all, 1 - c, 0), "c")
    table_full = in_order(c, pick(table_all, c, 0), rest, 1)
    table_full = table_full.reshape(2, strategies, wide).transpose(1, 0, 2).reshape(strategies, cols)
    table_grad = jnp.dot(mixing.T, table_full, precision=HIGHEST) * grad_scale

    parts = home.reshape(NC, 2, half, wide)
    back = jax.ShapeDtypeStruct(parts.shape[1:], BF)
    back = swap(call(take_body, (1 - c).reshape(1).astype(jnp.int32), (parts,), back, (table_sum,)), "c")
    proj = in_order(c, pick(parts, c, 0), back, 1).reshape(2, rows, wide)
    gating = 1.0 + rows_of(members(ids, strategies), table)
    proj = jnp.concatenate([proj[0], proj[1]], axis=1).astype(F32)
    layer_out = (residual.reshape(rows, cols).astype(F32) + proj * gating).astype(BF)

    head_grad = pick(head_grad, y, 0).astype(F32) + head_near[0].astype(F32) + head_near[1].astype(F32)

    shape = head_out.shape
    return layer_out.reshape(shape), head_grad.astype(BF).reshape(shape), weight_sum * grad_scale, table_grad


def solution(mesh):
    fine = Mesh(mesh.devices.reshape(XH, NY, NZ, XL, NC), ("xh", "y", "z", "xl", "c"))
    dp, mp = ("xh", "y", "z"), ("xl", "c")
    tokens = P(None, dp, mp)
    return jax.shard_map(
        on_device,
        mesh=fine,
        in_specs=(tokens, tokens, P(dp, mp), P(None, mp), P(), P(None, dp), tokens),
        out_specs=(tokens, tokens, P(dp, mp), P(None, mp)),
        check_vma=False,
    )
```

```python
import math

import jax
import jax.numpy as jnp
from jax import lax
from jax.experimental import pallas as pl
from jax.experimental.pallas import tpu as pltpu
from jax.sharding import Mesh, PartitionSpec as P

XH, NY, NZ, XL, NC = 2, 4, 8, 2, 2
BF = jnp.bfloat16
F32 = jnp.float32
HIGHEST = lax.Precision.HIGHEST


def swap(a, axis):
    return lax.ppermute(a, axis, [(0, 1), (1, 0)])


def exchange(a, axis):
    return lax.all_to_all(a, axis, 0, 0, tiled=True)


def spread(a, axis, n):
    return exchange(jnp.broadcast_to(a[None], (n,) + a.shape), axis)


def turn(a, k):
    return lax.ppermute(a, "y", [(i, (i + k) % NY) for i in range(NY)])


def gather_y(a, y):
    half = a.shape[1] // 2
    up, down = turn(a, 1), turn(a, -1)
    out = jnp.zeros((NY,) + a.shape, a.dtype)
    for piece, k in ((a, 0), (up, 1), (down, 3)):
        out = lax.dynamic_update_slice(out, piece[None], ((y - k) % NY, 0, 0))
    out = lax.dynamic_update_slice(out, turn(up[:, :half], 1)[None], ((y + 2) % NY, 0, 0))
    return lax.dynamic_update_slice(out, turn(down[:, half:], -1)[None], ((y + 2) % NY, 0, half))


def far_blocks(a, y):
    half = a.shape[2] // 2
    far = pick(a, (y + 2) % NY, 0)
    return turn(far[:, :half], 1), turn(far[:, half:], -1)


def near_blocks(a, far, y, after):
    block = jax.ShapeDtypeStruct(a.shape[1:], BF)
    up, down = call(pass_body, y.reshape(1).astype(jnp.int32), (a,) + far, (block, block), after)
    return turn(up, 1), turn(down, -1)


VMEM = pl.BlockSpec(memory_space=pltpu.VMEM)
SMEM = pl.BlockSpec(memory_space=pltpu.SMEM)
STEP = 256


TOKEN = jax.ShapeDtypeStruct((8, 128), F32)


def call(body, at, operands, out_shape, after=()):
    count = len(operands) + 1
    return pl.pallas_call(
        lambda *refs: body(*refs[:count], *refs[count + len(after) :]),
        out_shape=out_shape,
        in_specs=[SMEM] + [VMEM] * len(operands) + [pl.BlockSpec(memory_space=pl.ANY)] * len(after),
        out_specs=jax.tree.map(lambda _: VMEM, out_shape),
        compiler_params=pltpu.CompilerParams(vmem_limit_bytes=16 * 2**20),
        cost_estimate=pl.CostEstimate(flops=2**20, bytes_accessed=2**10, transcendentals=0),
    )(at, *operands, *after)


def call_token(body, at, operands, out_shape, after=()):
    def both(*refs):
        body(*refs[:-1])
        refs[-1][...] = jnp.zeros(refs[-1].shape, F32)

    return call(both, at, operands, (out_shape, TOKEN), after)


def pass_body(at, a, from_below, from_above, up, down):
    half = from_below.shape[1]
    above, below = lax.rem(at[0] + 1, NY), lax.rem(at[0] + NY - 1, NY)
    up[:, :half] = (a[above, :, :half].astype(F32) + from_below[...].astype(F32)).astype(BF)
    up[:, half:] = a[above, :, half:]
    down[:, :half] = a[below, :, :half]
    down[:, half:] = (a[below, :, half:].astype(F32) + from_above[...].astype(F32)).astype(BF)


def take_body(at, a, out):
    out[...] = a[at[0]]


def add_body(at, a, b, out):
    out[...] = (a[...].astype(F32) + b[...].astype(F32)).astype(out.dtype)


def pair_body(at, own, other, out):
    out[at[0]] = own[...]
    out[1 - at[0]] = other[...]


def split3(a):
    parts = []
    for _ in range(3):
        parts.append(a.astype(BF))
        a = a - parts[-1].astype(F32)
    return parts


def hot_of(got, k, rows, strategies):
    ids = got[k, rows : rows + 16, :].astype(F32)[:1, :rows]
    return (lax.broadcasted_iota(jnp.int32, (strategies, rows), 0).astype(F32) == ids).astype(BF)


def table_body(at, mixing, own, there, out):
    where = pl.ds(pl.multiple_of(at[1] * out.shape[1], 128), out.shape[1])
    table = jnp.where(at[0] == 1, own[:, where].astype(F32), there[:, where].astype(F32))
    out[...] = jnp.dot(mixing[...], table, precision=HIGHEST, preferred_element_type=F32)


def gate_body(at, got, table, out):
    rows = out.shape[0] // NY
    parts = split3(table[...])
    for k in range(NY):
        hot = hot_of(got, k, rows, table.shape[0])
        gating = jnp.ones((rows, out.shape[1]), F32)
        for part in reversed(parts):
            gating += lax.dot_general(hot, part, (((0,), (0,)), ((), ())), preferred_element_type=F32)
        out[k * rows : (k + 1) * rows, :] = (got[k, :rows, :].astype(F32) * gating).astype(BF)


def home_body(at, stay, away, home):
    home[...] = (stay[...] + away[...].astype(F32)).astype(BF)


def keep_body(at, ho, w, theirs, near, far, away, stay, table):
    rows, half = ho[:, at[1]].reshape(-1, ho.shape[-1]), ho.shape[2]
    hot = [hot_of(near, k, half, table.shape[1]) for k in range(NY)]
    for which, x, cot in ((0, at[0], near), (1, 1 - at[0], far)):
        for n in range(0, w.shape[1], STEP):
            span = slice(n, n + STEP)
            chip = lax.dot_general(rows, w[x, span, :], (((1,), (1,)), ((), ())), preferred_element_type=F32)
            chip = chip.astype(BF).astype(F32) + theirs[x, :, span].astype(F32)
            if which:
                away[:, span] = chip.astype(BF)
            else:
                stay[:, span] = chip
            total = jnp.zeros((table.shape[1], STEP), F32)
            for k in range(NY):
                for part in split3(cot[k, :half, span].astype(F32) * chip[k * half : (k + 1) * half]):
                    total += jnp.dot(hot[k], part, preferred_element_type=F32)
            table[which, :, span] = total


def project_body(at, ho, w, out):
    rows = ho[:, at[0]].reshape(-1, ho.shape[-1])
    for x in range(XL):
        for n in range(0, w.shape[1], STEP):
            out[x, :, n : n + STEP] = lax.dot_general(
                rows, w[x, n : n + STEP, :], (((1,), (1,)), ((), ())), preferred_element_type=F32
            ).astype(BF)


def weight_body(at, near, far, near_c, far_c, ho, out):
    xl, c = at[0], at[1]
    mine = ho[:, c].reshape(-1, ho.shape[-1])
    theirs = ho[:, 1 - c].reshape(-1, ho.shape[-1])
    over = (((0,), (0,)), ((), ()))
    for x, p, q in ((xl, near, near_c), (1 - xl, far, far_c)):
        for n in range(0, out.shape[-1], STEP):
            total = lax.dot_general(p[...], mine[:, n : n + STEP], over, preferred_element_type=F32)
            total += lax.dot_general(q[...], theirs[:, n : n + STEP], over, preferred_element_type=F32)
            out[x, :, n : n + STEP] = total.astype(BF)


def head_body(at, near, far, near_c, far_c, w, out):
    xl, c = at[0], at[1]
    for half, p, q in ((c, near, far), (1 - c, near_c, far_c)):
        for n in range(0, out.shape[-1], STEP):
            total = jnp.dot(p[...], w[xl, :, n : n + STEP], preferred_element_type=F32)
            total += jnp.dot(q[...], w[1 - xl, :, n : n + STEP], preferred_element_type=F32)
            out[:, half, :, n : n + STEP] = total.astype(BF).reshape(NY, -1, STEP)


def pick(a, at, dim):
    return lax.dynamic_index_in_dim(a, at, dim, keepdims=False)


def in_order(index, own, other, dim):
    first = jnp.where(index == 0, own, other)
    second = jnp.where(index == 0, other, own)
    return jnp.stack([first, second], axis=dim)


def mixture(meta_graph):
    counts = meta_graph.astype(F32)
    totals = jnp.maximum(jnp.sum(counts, axis=1, keepdims=True), 1.0)
    return jnp.eye(meta_graph.shape[0], dtype=F32) + counts / totals


def members(ids, strategies):
    return (lax.broadcasted_iota(jnp.int32, (strategies, 1), 0) == ids[None, :]).astype(F32)


def rows_of(one_hot, table):
    return lax.dot_general(one_hot, table, (((0,), (0,)), ((), ())), precision=HIGHEST, preferred_element_type=F32)


def on_device(head_out, residual, out_weight, strategy_table, meta_graph, strategy_ids, cotangent):
    batches, local_rows, cols = head_out.shape
    rows, half, wide = batches * local_rows, batches * local_rows // 2, cols // 2
    strategies = meta_graph.shape[0]
    wr = out_weight.shape[0]
    pad = 16
    xh, y, xl, c = (lax.axis_index(name) for name in ("xh", "y", "xl", "c"))
    grad_scale = 1.0 / math.sqrt(rows * XH * NY * NZ)

    ho = head_out.reshape(rows, cols)
    cot = cotangent.reshape(rows, cols)
    ids = strategy_ids.reshape(rows)

    cot_parts = cot.reshape(NC, half, cols)
    other = swap(pick(cot_parts, 1 - c, 0), "c")
    mine = in_order(c, pick(cot_parts, c, 0), other, 0)
    by_y = mine.reshape(NC, half, 2, wide).transpose(0, 2, 1, 3).reshape(NY, half, wide)
    tag = pick(ids.reshape(NC, half), c, 0).astype(BF)
    tag = jnp.broadcast_to(jnp.pad(tag, (0, wide - half))[None, None], (NY, pad, wide))
    got = exchange(jnp.concatenate([by_y, tag], axis=1), "y")

    ho_y = gather_y(ho, y).reshape(NY, NC, half, cols)

    unit = call(
        pair_body,
        xh.reshape(1).astype(jnp.int32),
        (out_weight, swap(out_weight, "xh")),
        jax.ShapeDtypeStruct((XH,) + out_weight.shape, BF),
        (other,),
    )
    weight = lax.all_gather(unit, "z", axis=1, tiled=True)

    mixing = mixture(meta_graph)
    table = jnp.dot(mixing, strategy_table.astype(F32), precision=HIGHEST)
    there = swap(strategy_table, "c")
    source = jnp.stack([(y // 2 == c).astype(jnp.int32), (y % 2).astype(jnp.int32)])
    table_y = call(table_body, source, (mixing, strategy_table, there), jax.ShapeDtypeStruct((strategies, wide), F32))
    gate = lambda block, table: call(gate_body, source, (block, table), jax.ShapeDtypeStruct((NY * half, wide), BF))
    got_far = swap(got, "xl")

    near, far = gate(got, table_y), gate(got_far, swap(table_y, "xl"))
    pieces = (near, far, swap(near, "c"), swap(far, "c"))
    at = jnp.stack([xl, c]).astype(jnp.int32)

    give, given = call_token(
        project_body,
        (1 - c).reshape(1).astype(jnp.int32),
        (ho_y, weight),
        jax.ShapeDtypeStruct((XL, NY * half, wide), BF),
        (far, near),
    )
    theirs = swap(give, "c")
    wg, weighed = call_token(weight_body, at, pieces + (ho_y,), jax.ShapeDtypeStruct((XH, NZ * wr, cols), BF), (given,))
    head_grad, headed = call_token(
        head_body, at, pieces + (weight,), jax.ShapeDtypeStruct((NY, NC, half, cols), BF), (weighed,)
    )
    head_grad = head_grad.reshape(NY, rows, cols)
    head_far = far_blocks(head_grad, y)
    away, stay, table_part = call(
        keep_body,
        at,
        (ho_y, weight, theirs, got, got_far),
        (
            jax.ShapeDtypeStruct((NY * half, wide), BF),
            jax.ShapeDtypeStruct((NY * half, wide), F32),
            jax.ShapeDtypeStruct((XL, strategies, wide), F32),
        ),
        (headed,),
    )

    wg_part = lax.psum_scatter(wg, "z", scatter_dimension=1, tiled=True)
    wg_other = swap(pick(wg_part, 1 - xh, 0), "xh")
    weight_sum = pick(wg_part, xh, 0).astype(F32) + wg_other.astype(F32)

    table_part = table_part.reshape(XL, NC, strategies // NC, wide)
    sent = (pick(table_part, c, 1) + swap(pick(table_part, 1 - c, 1), "c")).astype(BF)
    head_near = near_blocks(head_grad, head_far, y, (sent,))
    beside = lambda a, bit: lax.ppermute(a, "z", [(i, i ^ bit) for i in range(NZ)])
    sent = (sent.astype(F32) + beside(sent, 1).astype(F32)).astype(BF)
    sent = (sent.astype(F32) + beside(sent, 2).astype(F32)).astype(BF)
    home = jax.ShapeDtypeStruct(away.shape, BF)
    home = call(home_body, at, (stay, swap(away, "xl")), home, head_near + (sent,))
    table_sum = call(add_body, at, (sent, beside(sent, 4)), jax.ShapeDtypeStruct(sent.shape, F32), (home,))
    home = exchange(home.reshape(NY, half, wide), "y")
    table_sum = table_sum[0] + swap(table_sum[1], "xl")
    table_sum = call(
        add_body, at, (table_sum, swap(table_sum, "xh")), jax.ShapeDtypeStruct(table_sum.shape, F32), (home, wg_other)
    )
    table_all = spread(table_sum, "y", NY).reshape(NC, 2, strategies // NC, wide)
    rest = swap(pick(table_all, 1 - c, 0), "c")
    table_full = in_order(c, pick(table_all, c, 0), rest, 1)
    table_full = table_full.reshape(2, strategies, wide).transpose(1, 0, 2).reshape(strategies, cols)
    table_grad = jnp.dot(mixing.T, table_full, precision=HIGHEST) * grad_scale

    parts = home.reshape(NC, 2, half, wide)
    back = jax.ShapeDtypeStruct(parts.shape[1:], BF)
    back = swap(call(take_body, (1 - c).reshape(1).astype(jnp.int32), (parts,), back, (table_sum,)), "c")
    proj = in_order(c, pick(parts, c, 0), back, 1).reshape(2, rows, wide)
    gating = 1.0 + rows_of(members(ids, strategies), table)
    proj = jnp.concatenate([proj[0], proj[1]], axis=1).astype(F32)
    layer_out = (residual.reshape(rows, cols).astype(F32) + proj * gating).astype(BF)

    head_grad = pick(head_grad, y, 0).astype(F32) + head_near[0].astype(F32) + head_near[1].astype(F32)

    shape = head_out.shape
    return layer_out.reshape(shape), head_grad.astype(BF).reshape(shape), weight_sum * grad_scale, table_grad


def solution(mesh):
    fine = Mesh(mesh.devices.reshape(XH, NY, NZ, XL, NC), ("xh", "y", "z", "xl", "c"))
    dp, mp = ("xh", "y", "z"), ("xl", "c")
    tokens = P(None, dp, mp)
    return jax.shard_map(
        on_device,
        mesh=fine,
        in_specs=(tokens, tokens, P(dp, mp), P(None, mp), P(), P(None, dp), tokens),
        out_specs=(tokens, tokens, P(dp, mp), P(None, mp)),
        check_vma=False,
    )
```

```python
import math

import jax
import jax.numpy as jnp
from jax import lax
from jax.experimental import pallas as pl
from jax.experimental.pallas import tpu as pltpu
from jax.sharding import Mesh, PartitionSpec as P

XH, NY, NZ, XL, NC = 2, 4, 8, 2, 2
BF = jnp.bfloat16
F32 = jnp.float32
HIGHEST = lax.Precision.HIGHEST


def swap(a, axis):
    return lax.ppermute(a, axis, [(0, 1), (1, 0)])


def exchange(a, axis):
    return lax.all_to_all(a, axis, 0, 0, tiled=True)


def spread(a, axis, n):
    return exchange(jnp.broadcast_to(a[None], (n,) + a.shape), axis)


def turn(a, k):
    return lax.ppermute(a, "y", [(i, (i + k) % NY) for i in range(NY)])


def gather_y(a, y):
    half = a.shape[1] // 2
    up, down = turn(a, 1), turn(a, -1)
    out = jnp.zeros((NY,) + a.shape, a.dtype)
    for piece, k in ((a, 0), (up, 1), (down, 3)):
        out = lax.dynamic_update_slice(out, piece[None], ((y - k) % NY, 0, 0))
    out = lax.dynamic_update_slice(out, turn(up[:, :half], 1)[None], ((y + 2) % NY, 0, 0))
    return lax.dynamic_update_slice(out, turn(down[:, half:], -1)[None], ((y + 2) % NY, 0, half))


def far_blocks(a, y):
    half = a.shape[2] // 2
    far = pick(a, (y + 2) % NY, 0)
    return turn(far[:, :half], 1), turn(far[:, half:], -1)


def near_blocks(a, far, y, after):
    block = jax.ShapeDtypeStruct(a.shape[1:], BF)
    up, down = call(pass_body, y.reshape(1).astype(jnp.int32), (a,) + far, (block, block), after)
    return turn(up, 1), turn(down, -1)


VMEM = pl.BlockSpec(memory_space=pltpu.VMEM)
SMEM = pl.BlockSpec(memory_space=pltpu.SMEM)
STEP = 256


TOKEN = jax.ShapeDtypeStruct((8, 128), F32)


def call(body, at, operands, out_shape, after=()):
    count = len(operands) + 1
    return pl.pallas_call(
        lambda *refs: body(*refs[:count], *refs[count + len(after) :]),
        out_shape=out_shape,
        in_specs=[SMEM] + [VMEM] * len(operands) + [pl.BlockSpec(memory_space=pl.ANY)] * len(after),
        out_specs=jax.tree.map(lambda _: VMEM, out_shape),
        compiler_params=pltpu.CompilerParams(vmem_limit_bytes=16 * 2**20),
        cost_estimate=pl.CostEstimate(flops=2**20, bytes_accessed=2**10, transcendentals=0),
    )(at, *operands, *after)


def call_token(body, at, operands, out_shape, after=()):
    def both(*refs):
        body(*refs[:-1])
        refs[-1][...] = jnp.zeros(refs[-1].shape, F32)

    return call(both, at, operands, (out_shape, TOKEN), after)


def pass_body(at, a, from_below, from_above, up, down):
    half = from_below.shape[1]
    above, below = lax.rem(at[0] + 1, NY), lax.rem(at[0] + NY - 1, NY)
    up[:, :half] = (a[above, :, :half].astype(F32) + from_below[...].astype(F32)).astype(BF)
    up[:, half:] = a[above, :, half:]
    down[:, :half] = a[below, :, :half]
    down[:, half:] = (a[below, :, half:].astype(F32) + from_above[...].astype(F32)).astype(BF)


def copy_body(at, a, out):
    out[...] = a[...]


def take_body(at, a, out):
    out[...] = a[at[0]]


def add_body(at, a, b, out):
    out[...] = (a[...].astype(F32) + b[...].astype(F32)).astype(out.dtype)


def pair_body(at, own, other, out):
    out[at[0]] = own[...]
    out[1 - at[0]] = other[...]


def split3(a):
    parts = []
    for _ in range(3):
        parts.append(a.astype(BF))
        a = a - parts[-1].astype(F32)
    return parts


def hot_of(got, k, rows, strategies):
    ids = got[k, rows : rows + 16, :].astype(F32)[:1, :rows]
    return (lax.broadcasted_iota(jnp.int32, (strategies, rows), 0).astype(F32) == ids).astype(BF)


def table_body(at, mixing, own, there, out):
    where = pl.ds(pl.multiple_of(at[1] * out.shape[1], 128), out.shape[1])
    table = jnp.where(at[0] == 1, own[:, where].astype(F32), there[:, where].astype(F32))
    out[...] = jnp.dot(mixing[...], table, precision=HIGHEST, preferred_element_type=F32)


def gate_body(at, got, table, out):
    rows = out.shape[0] // NY
    parts = split3(table[...])
    for k in range(NY):
        hot = hot_of(got, k, rows, table.shape[0])
        gating = jnp.ones((rows, out.shape[1]), F32)
        for part in reversed(parts):
            gating += lax.dot_general(hot, part, (((0,), (0,)), ((), ())), preferred_element_type=F32)
        out[k * rows : (k + 1) * rows, :] = (got[k, :rows, :].astype(F32) * gating).astype(BF)


def home_body(at, stay, away, home):
    home[...] = (stay[...] + away[...].astype(F32)).astype(BF)


def keep_body(at, ho, w, theirs, near, far, away, stay, table):
    rows, half = ho[:, at[1]].reshape(-1, ho.shape[-1]), ho.shape[2]
    hot = [hot_of(near, k, half, table.shape[1]) for k in range(NY)]
    for which, x, cot in ((0, at[0], near), (1, 1 - at[0], far)):
        for n in range(0, w.shape[1], STEP):
            span = slice(n, n + STEP)
            chip = lax.dot_general(rows, w[x, span, :], (((1,), (1,)), ((), ())), preferred_element_type=F32)
            chip = chip.astype(BF).astype(F32) + theirs[x, :, span].astype(F32)
            if which:
                away[:, span] = chip.astype(BF)
            else:
                stay[:, span] = chip
            total = jnp.zeros((table.shape[1], STEP), F32)
            for k in range(NY):
                for part in split3(cot[k, :half, span].astype(F32) * chip[k * half : (k + 1) * half]):
                    total += jnp.dot(hot[k], part, preferred_element_type=F32)
            table[which, :, span] = total


def project_body(at, ho, w, out):
    rows = ho[:, at[0]].reshape(-1, ho.shape[-1])
    for x in range(XL):
        for n in range(0, w.shape[1], STEP):
            out[x, :, n : n + STEP] = lax.dot_general(
                rows, w[x, n : n + STEP, :], (((1,), (1,)), ((), ())), preferred_element_type=F32
            ).astype(BF)


def weight_body(at, near, far, near_c, far_c, ho, out):
    xl, c = at[0], at[1]
    mine = ho[:, c].reshape(-1, ho.shape[-1])
    theirs = ho[:, 1 - c].reshape(-1, ho.shape[-1])
    over = (((0,), (0,)), ((), ()))
    for x, p, q in ((xl, near, near_c), (1 - xl, far, far_c)):
        for n in range(0, out.shape[-1], STEP):
            total = lax.dot_general(p[...], mine[:, n : n + STEP], over, preferred_element_type=F32)
            total += lax.dot_general(q[...], theirs[:, n : n + STEP], over, preferred_element_type=F32)
            out[x, :, n : n + STEP] = total.astype(BF)


def head_body(at, near, far, near_c, far_c, w, out):
    xl, c = at[0], at[1]
    for half, p, q in ((c, near, far), (1 - c, near_c, far_c)):
        for n in range(0, out.shape[-1], STEP):
            total = jnp.dot(p[...], w[xl, :, n : n + STEP], preferred_element_type=F32)
            total += jnp.dot(q[...], w[1 - xl, :, n : n + STEP], preferred_element_type=F32)
            out[:, half, :, n : n + STEP] = total.astype(BF).reshape(NY, -1, STEP)


def pick(a, at, dim):
    return lax.dynamic_index_in_dim(a, at, dim, keepdims=False)


def in_order(index, own, other, dim):
    first = jnp.where(index == 0, own, other)
    second = jnp.where(index == 0, other, own)
    return jnp.stack([first, second], axis=dim)


def mixture(meta_graph):
    counts = meta_graph.astype(F32)
    totals = jnp.maximum(jnp.sum(counts, axis=1, keepdims=True), 1.0)
    return jnp.eye(meta_graph.shape[0], dtype=F32) + counts / totals


def members(ids, strategies):
    return (lax.broadcasted_iota(jnp.int32, (strategies, 1), 0) == ids[None, :]).astype(F32)


def rows_of(one_hot, table):
    return lax.dot_general(one_hot, table, (((0,), (0,)), ((), ())), precision=HIGHEST, preferred_element_type=F32)


def on_device(head_out, residual, out_weight, strategy_table, meta_graph, strategy_ids, cotangent):
    batches, local_rows, cols = head_out.shape
    rows, half, wide = batches * local_rows, batches * local_rows // 2, cols // 2
    strategies = meta_graph.shape[0]
    wr = out_weight.shape[0]
    pad = 16
    xh, y, xl, c = (lax.axis_index(name) for name in ("xh", "y", "xl", "c"))
    grad_scale = 1.0 / math.sqrt(rows * XH * NY * NZ)

    ho = head_out.reshape(rows, cols)
    cot = cotangent.reshape(rows, cols)
    ids = strategy_ids.reshape(rows)

    cot_parts = cot.reshape(NC, half, cols)
    other = swap(pick(cot_parts, 1 - c, 0), "c")
    mine = in_order(c, pick(cot_parts, c, 0), other, 0)
    by_y = mine.reshape(NC, half, 2, wide).transpose(0, 2, 1, 3).reshape(NY, half, wide)
    tag = pick(ids.reshape(NC, half), c, 0).astype(BF)
    tag = jnp.broadcast_to(jnp.pad(tag, (0, wide - half))[None, None], (NY, pad, wide))
    got = exchange(jnp.concatenate([by_y, tag], axis=1), "y")

    ho_y = gather_y(ho, y).reshape(NY, NC, half, cols)

    unit = call(
        pair_body,
        xh.reshape(1).astype(jnp.int32),
        (out_weight, swap(out_weight, "xh")),
        jax.ShapeDtypeStruct((XH,) + out_weight.shape, BF),
        (other,),
    )
    weight = lax.all_gather(unit, "z", axis=1, tiled=True)

    mixing = mixture(meta_graph)
    table = jnp.dot(mixing, strategy_table.astype(F32), precision=HIGHEST)
    there = swap(strategy_table, "c")
    source = jnp.stack([(y // 2 == c).astype(jnp.int32), (y % 2).astype(jnp.int32)])
    table_y = call(table_body, source, (mixing, strategy_table, there), jax.ShapeDtypeStruct((strategies, wide), F32))
    gate = lambda block, table: call(gate_body, source, (block, table), jax.ShapeDtypeStruct((NY * half, wide), BF))
    got_far = swap(got, "xl")

    near = gate(got, table_y)
    table_out = call(copy_body, source, (table_y,), jax.ShapeDtypeStruct(table_y.shape, F32), (near,))
    far = gate(got_far, swap(table_out, "xl"))
    pieces = (near, far, swap(near, "c"), swap(far, "c"))
    at = jnp.stack([xl, c]).astype(jnp.int32)

    give, given = call_token(
        project_body,
        (1 - c).reshape(1).astype(jnp.int32),
        (ho_y, weight),
        jax.ShapeDtypeStruct((XL, NY * half, wide), BF),
        (far, near),
    )
    theirs = swap(give, "c")
    wg, weighed = call_token(weight_body, at, pieces + (ho_y,), jax.ShapeDtypeStruct((XH, NZ * wr, cols), BF), (given,))
    head_grad, headed = call_token(
        head_body, at, pieces + (weight,), jax.ShapeDtypeStruct((NY, NC, half, cols), BF), (weighed,)
    )
    head_grad = head_grad.reshape(NY, rows, cols)
    head_far = far_blocks(head_grad, y)
    away, stay, table_part = call(
        keep_body,
        at,
        (ho_y, weight, theirs, got, got_far),
        (
            jax.ShapeDtypeStruct((NY * half, wide), BF),
            jax.ShapeDtypeStruct((NY * half, wide), F32),
            jax.ShapeDtypeStruct((XL, strategies, wide), F32),
        ),
        (headed,),
    )

    wg_part = lax.psum_scatter(wg, "z", scatter_dimension=1, tiled=True)
    wg_other = swap(pick(wg_part, 1 - xh, 0), "xh")
    weight_sum = pick(wg_part, xh, 0).astype(F32) + wg_other.astype(F32)

    table_part = table_part.reshape(XL, NC, strategies // NC, wide)
    sent = (pick(table_part, c, 1) + swap(pick(table_part, 1 - c, 1), "c")).astype(BF)
    head_near = near_blocks(head_grad, head_far, y, (sent,))
    beside = lambda a, bit: lax.ppermute(a, "z", [(i, i ^ bit) for i in range(NZ)])
    sent = (sent.astype(F32) + beside(sent, 1).astype(F32)).astype(BF)
    sent = (sent.astype(F32) + beside(sent, 2).astype(F32)).astype(BF)
    home = jax.ShapeDtypeStruct(away.shape, BF)
    home = call(home_body, at, (stay, swap(away, "xl")), home, head_near + (sent,))
    table_sum = call(add_body, at, (sent, beside(sent, 4)), jax.ShapeDtypeStruct(sent.shape, F32), (home,))
    home = exchange(home.reshape(NY, half, wide), "y")
    table_sum = table_sum[0] + swap(table_sum[1], "xl")
    table_sum = call(
        add_body, at, (table_sum, swap(table_sum, "xh")), jax.ShapeDtypeStruct(table_sum.shape, F32), (home, wg_other)
    )
    table_all = spread(table_sum, "y", NY).reshape(NC, 2, strategies // NC, wide)
    rest = swap(pick(table_all, 1 - c, 0), "c")
    table_full = in_order(c, pick(table_all, c, 0), rest, 1)
    table_full = table_full.reshape(2, strategies, wide).transpose(1, 0, 2).reshape(strategies, cols)
    table_grad = jnp.dot(mixing.T, table_full, precision=HIGHEST) * grad_scale

    parts = home.reshape(NC, 2, half, wide)
    back = jax.ShapeDtypeStruct(parts.shape[1:], BF)
    back = swap(call(take_body, (1 - c).reshape(1).astype(jnp.int32), (parts,), back, (table_sum,)), "c")
    proj = in_order(c, pick(parts, c, 0), back, 1).reshape(2, rows, wide)
    gating = 1.0 + rows_of(members(ids, strategies), table)
    proj = jnp.concatenate([proj[0], proj[1]], axis=1).astype(F32)
    layer_out = (residual.reshape(rows, cols).astype(F32) + proj * gating).astype(BF)

    head_grad = pick(head_grad, y, 0).astype(F32) + head_near[0].astype(F32) + head_near[1].astype(F32)

    shape = head_out.shape
    return layer_out.reshape(shape), head_grad.astype(BF).reshape(shape), weight_sum * grad_scale, table_grad


def solution(mesh):
    fine = Mesh(mesh.devices.reshape(XH, NY, NZ, XL, NC), ("xh", "y", "z", "xl", "c"))
    dp, mp = ("xh", "y", "z"), ("xl", "c")
    tokens = P(None, dp, mp)
    return jax.shard_map(
        on_device,
        mesh=fine,
        in_specs=(tokens, tokens, P(dp, mp), P(None, mp), P(), P(None, dp), tokens),
        out_specs=(tokens, tokens, P(dp, mp), P(None, mp)),
        check_vma=False,
    )
```

```python
import math

import jax
import jax.numpy as jnp
from jax import lax
from jax.experimental import pallas as pl
from jax.experimental.pallas import tpu as pltpu
from jax.sharding import Mesh, PartitionSpec as P

XH, NY, NZ, XL, NC = 2, 4, 8, 2, 2
BF = jnp.bfloat16
F32 = jnp.float32
HIGHEST = lax.Precision.HIGHEST


def swap(a, axis):
    return lax.ppermute(a, axis, [(0, 1), (1, 0)])


def exchange(a, axis):
    return lax.all_to_all(a, axis, 0, 0, tiled=True)


def spread(a, axis, n):
    return exchange(jnp.broadcast_to(a[None], (n,) + a.shape), axis)


def turn(a, k):
    return lax.ppermute(a, "y", [(i, (i + k) % NY) for i in range(NY)])


def gather_y(a, y):
    half = a.shape[1] // 2
    up, down = turn(a, 1), turn(a, -1)
    out = jnp.zeros((NY,) + a.shape, a.dtype)
    for piece, k in ((a, 0), (up, 1), (down, 3)):
        out = lax.dynamic_update_slice(out, piece[None], ((y - k) % NY, 0, 0))
    out = lax.dynamic_update_slice(out, turn(up[:, :half], 1)[None], ((y + 2) % NY, 0, 0))
    return lax.dynamic_update_slice(out, turn(down[:, half:], -1)[None], ((y + 2) % NY, 0, half))


def far_blocks(a, y):
    half = a.shape[2] // 2
    far = pick(a, (y + 2) % NY, 0)
    return turn(far[:, :half], 1), turn(far[:, half:], -1)


def near_blocks(a, far, y, after):
    block = jax.ShapeDtypeStruct(a.shape[1:], BF)
    up, down = call(pass_body, y.reshape(1).astype(jnp.int32), (a,) + far, (block, block), after)
    return turn(up, 1), turn(down, -1)


VMEM = pl.BlockSpec(memory_space=pltpu.VMEM)
SMEM = pl.BlockSpec(memory_space=pltpu.SMEM)
STEP = 256


TOKEN = jax.ShapeDtypeStruct((8, 128), F32)


def call(body, at, operands, out_shape, after=()):
    count = len(operands) + 1
    return pl.pallas_call(
        lambda *refs: body(*refs[:count], *refs[count + len(after) :]),
        out_shape=out_shape,
        in_specs=[SMEM] + [VMEM] * len(operands) + [pl.BlockSpec(memory_space=pl.ANY)] * len(after),
        out_specs=jax.tree.map(lambda _: VMEM, out_shape),
        compiler_params=pltpu.CompilerParams(vmem_limit_bytes=16 * 2**20),
        cost_estimate=pl.CostEstimate(flops=2**20, bytes_accessed=2**10, transcendentals=0),
    )(at, *operands, *after)


def call_token(body, at, operands, out_shape, after=()):
    def both(*refs):
        body(*refs[:-1])
        refs[-1][...] = jnp.zeros(refs[-1].shape, F32)

    return call(both, at, operands, (out_shape, TOKEN), after)


def pass_body(at, a, from_below, from_above, up, down):
    half = from_below.shape[1]
    above, below = lax.rem(at[0] + 1, NY), lax.rem(at[0] + NY - 1, NY)
    up[:, :half] = (a[above, :, :half].astype(F32) + from_below[...].astype(F32)).astype(BF)
    up[:, half:] = a[above, :, half:]
    down[:, :half] = a[below, :, :half]
    down[:, half:] = (a[below, :, half:].astype(F32) + from_above[...].astype(F32)).astype(BF)


def copy_body(at, a, out):
    out[...] = a[...]


def take_body(at, a, out):
    out[...] = a[at[0]]


def add_body(at, a, b, out):
    out[...] = (a[...].astype(F32) + b[...].astype(F32)).astype(out.dtype)


def pair_body(at, own, other, out):
    out[at[0]] = own[...]
    out[1 - at[0]] = other[...]


def split3(a):
    parts = []
    for _ in range(3):
        parts.append(a.astype(BF))
        a = a - parts[-1].astype(F32)
    return parts


def hot_of(got, k, rows, strategies):
    ids = got[k, rows : rows + 16, :].astype(F32)[:1, :rows]
    return (lax.broadcasted_iota(jnp.int32, (strategies, rows), 0).astype(F32) == ids).astype(BF)


def table_body(at, mixing, own, there, out):
    where = pl.ds(pl.multiple_of(at[1] * out.shape[1], 128), out.shape[1])
    table = jnp.where(at[0] == 1, own[:, where].astype(F32), there[:, where].astype(F32))
    out[...] = jnp.dot(mixing[...], table, precision=HIGHEST, preferred_element_type=F32)


def gate_body(at, got, table, out):
    rows = out.shape[0] // NY
    parts = split3(table[...])
    for k in range(NY):
        hot = hot_of(got, k, rows, table.shape[0])
        gating = jnp.ones((rows, out.shape[1]), F32)
        for part in reversed(parts):
            gating += lax.dot_general(hot, part, (((0,), (0,)), ((), ())), preferred_element_type=F32)
        out[k * rows : (k + 1) * rows, :] = (got[k, :rows, :].astype(F32) * gating).astype(BF)


def home_body(at, stay, away, home):
    home[...] = (stay[...] + away[...].astype(F32)).astype(BF)


def keep_body(at, ho, w, theirs, near, far, away, stay, table):
    rows, half = ho[:, at[1]].reshape(-1, ho.shape[-1]), ho.shape[2]
    hot = [hot_of(near, k, half, table.shape[1]) for k in range(NY)]
    for which, x, cot in ((0, at[0], near), (1, 1 - at[0], far)):
        for n in range(0, w.shape[1], STEP):
            span = slice(n, n + STEP)
            chip = lax.dot_general(rows, w[x, span, :], (((1,), (1,)), ((), ())), preferred_element_type=F32)
            chip = chip.astype(BF).astype(F32) + theirs[x, :, span].astype(F32)
            if which:
                away[:, span] = chip.astype(BF)
            else:
                stay[:, span] = chip
            total = jnp.zeros((table.shape[1], STEP), F32)
            for k in range(NY):
                for part in split3(cot[k, :half, span].astype(F32) * chip[k * half : (k + 1) * half]):
                    total += jnp.dot(hot[k], part, preferred_element_type=F32)
            table[which, :, span] = total


def project_body(at, ho, w, out):
    rows = ho[:, at[0]].reshape(-1, ho.shape[-1])
    for x in range(XL):
        for n in range(0, w.shape[1], STEP):
            out[x, :, n : n + STEP] = lax.dot_general(
                rows, w[x, n : n + STEP, :], (((1,), (1,)), ((), ())), preferred_element_type=F32
            ).astype(BF)


def weight_body(at, near, far, near_c, far_c, ho, out):
    xl, c = at[0], at[1]
    mine = ho[:, c].reshape(-1, ho.shape[-1])
    theirs = ho[:, 1 - c].reshape(-1, ho.shape[-1])
    over = (((0,), (0,)), ((), ()))
    for x, p, q in ((xl, near, near_c), (1 - xl, far, far_c)):
        for n in range(0, out.shape[-1], STEP):
            total = lax.dot_general(p[...], mine[:, n : n + STEP], over, preferred_element_type=F32)
            total += lax.dot_general(q[...], theirs[:, n : n + STEP], over, preferred_element_type=F32)
            out[x, :, n : n + STEP] = total.astype(BF)


def head_body(at, near, far, near_c, far_c, w, out):
    xl, c = at[0], at[1]
    for half, p, q in ((c, near, far), (1 - c, near_c, far_c)):
        for n in range(0, out.shape[-1], STEP):
            total = jnp.dot(p[...], w[xl, :, n : n + STEP], preferred_element_type=F32)
            total += jnp.dot(q[...], w[1 - xl, :, n : n + STEP], preferred_element_type=F32)
            out[:, half, :, n : n + STEP] = total.astype(BF).reshape(NY, -1, STEP)


def pick(a, at, dim):
    return lax.dynamic_index_in_dim(a, at, dim, keepdims=False)


def in_order(index, own, other, dim):
    first = jnp.where(index == 0, own, other)
    second = jnp.where(index == 0, other, own)
    return jnp.stack([first, second], axis=dim)


def mixture(meta_graph):
    counts = meta_graph.astype(F32)
    totals = jnp.maximum(jnp.sum(counts, axis=1, keepdims=True), 1.0)
    return jnp.eye(meta_graph.shape[0], dtype=F32) + counts / totals


def members(ids, strategies):
    return (lax.broadcasted_iota(jnp.int32, (strategies, 1), 0) == ids[None, :]).astype(F32)


def rows_of(one_hot, table):
    return lax.dot_general(one_hot, table, (((0,), (0,)), ((), ())), precision=HIGHEST, preferred_element_type=F32)


def on_device(head_out, residual, out_weight, strategy_table, meta_graph, strategy_ids, cotangent):
    batches, local_rows, cols = head_out.shape
    rows, half, wide = batches * local_rows, batches * local_rows // 2, cols // 2
    strategies = meta_graph.shape[0]
    wr = out_weight.shape[0]
    pad = 16
    xh, y, xl, c = (lax.axis_index(name) for name in ("xh", "y", "xl", "c"))
    grad_scale = 1.0 / math.sqrt(rows * XH * NY * NZ)

    ho = head_out.reshape(rows, cols)
    cot = cotangent.reshape(rows, cols)
    ids = strategy_ids.reshape(rows)

    cot_parts = cot.reshape(NC, half, cols)
    other = swap(pick(cot_parts, 1 - c, 0), "c")
    mine = in_order(c, pick(cot_parts, c, 0), other, 0)
    by_y = mine.reshape(NC, half, 2, wide).transpose(0, 2, 1, 3).reshape(NY, half, wide)
    tag = pick(ids.reshape(NC, half), c, 0).astype(BF)
    tag = jnp.broadcast_to(jnp.pad(tag, (0, wide - half))[None, None], (NY, pad, wide))
    got = exchange(jnp.concatenate([by_y, tag], axis=1), "y")

    ho_y = gather_y(ho, y).reshape(NY, NC, half, cols)

    unit = call(
        pair_body,
        xh.reshape(1).astype(jnp.int32),
        (out_weight, swap(out_weight, "xh")),
        jax.ShapeDtypeStruct((XH,) + out_weight.shape, BF),
        (other,),
    )
    weight = lax.all_gather(unit, "z", axis=1, tiled=True)

    mixing = mixture(meta_graph)
    table = jnp.dot(mixing, strategy_table.astype(F32), precision=HIGHEST)
    there = swap(strategy_table, "c")
    source = jnp.stack([(y // 2 == c).astype(jnp.int32), (y % 2).astype(jnp.int32)])
    table_y = call(table_body, source, (mixing, strategy_table, there), jax.ShapeDtypeStruct((strategies, wide), F32))
    gate = lambda block, table: call(gate_body, source, (block, table), jax.ShapeDtypeStruct((NY * half, wide), BF))
    got_far = swap(got, "xl")

    near = gate(got, table_y)
    table_out = call(copy_body, source, (table_y,), jax.ShapeDtypeStruct(table_y.shape, F32), (near,))
    far = gate(got_far, swap(table_out, "xl"))
    pieces = (near, far, swap(near, "c"), swap(far, "c"))
    at = jnp.stack([xl, c]).astype(jnp.int32)

    give, given = call_token(
        project_body,
        (1 - c).reshape(1).astype(jnp.int32),
        (ho_y, weight),
        jax.ShapeDtypeStruct((XL, NY * half, wide), BF),
        (far, near),
    )
    theirs = swap(give, "c")
    wg, weighed = call_token(weight_body, at, pieces + (ho_y,), jax.ShapeDtypeStruct((XH, NZ * wr, cols), BF), (given,))
    head_grad, headed = call_token(
        head_body, at, pieces + (weight,), jax.ShapeDtypeStruct((NY, NC, half, cols), BF), (weighed,)
    )
    head_grad = head_grad.reshape(NY, rows, cols)
    head_far = far_blocks(head_grad, y)
    away, stay, table_part = call(
        keep_body,
        at,
        (ho_y, weight, theirs, got, got_far),
        (
            jax.ShapeDtypeStruct((NY * half, wide), BF),
            jax.ShapeDtypeStruct((NY * half, wide), F32),
            jax.ShapeDtypeStruct((XL, strategies, wide), F32),
        ),
        (headed,),
    )

    wg_part = lax.psum_scatter(wg, "z", scatter_dimension=1, tiled=True)
    wg_other = swap(pick(wg_part, 1 - xh, 0), "xh")
    weight_sum = pick(wg_part, xh, 0).astype(F32) + wg_other.astype(F32)

    table_part = table_part.reshape(XL, NC, strategies // NC, wide)
    sent = (pick(table_part, c, 1) + swap(pick(table_part, 1 - c, 1), "c")).astype(BF)
    head_near = near_blocks(head_grad, head_far, y, (sent,))
    beside = lambda a, bit: lax.ppermute(a, "z", [(i, i ^ bit) for i in range(NZ)])
    sent = (sent.astype(F32) + beside(sent, 1).astype(F32)).astype(BF)
    sent = (sent.astype(F32) + beside(sent, 2).astype(F32)).astype(BF)
    home = jax.ShapeDtypeStruct(away.shape, BF)
    home = call(home_body, at, (stay, swap(away, "xl")), home, head_near + (sent,))
    table_sum = call(add_body, at, (sent, beside(sent, 4)), jax.ShapeDtypeStruct(sent.shape, F32), (home,))
    home = exchange(home.reshape(NY, half, wide), "y")
    table_sum = table_sum[0] + swap(table_sum[1], "xl")
    table_sum = call(
        add_body, at, (table_sum, swap(table_sum, "xh")), jax.ShapeDtypeStruct(table_sum.shape, F32), (home, wg_other)
    )
    table_all = spread(table_sum.astype(BF), "y", NY).reshape(NC, 2, strategies // NC, wide)
    rest = swap(pick(table_all, 1 - c, 0), "c")
    table_full = in_order(c, pick(table_all, c, 0), rest, 1)
    table_full = table_full.astype(F32).reshape(2, strategies, wide).transpose(1, 0, 2).reshape(strategies, cols)
    table_grad = jnp.dot(mixing.T, table_full, precision=HIGHEST) * grad_scale

    parts = home.reshape(NC, 2, half, wide)
    back = jax.ShapeDtypeStruct(parts.shape[1:], BF)
    back = swap(call(take_body, (1 - c).reshape(1).astype(jnp.int32), (parts,), back, (table_sum,)), "c")
    proj = in_order(c, pick(parts, c, 0), back, 1).reshape(2, rows, wide)
    gating = 1.0 + rows_of(members(ids, strategies), table)
    proj = jnp.concatenate([proj[0], proj[1]], axis=1).astype(F32)
    layer_out = (residual.reshape(rows, cols).astype(F32) + proj * gating).astype(BF)

    head_grad = pick(head_grad, y, 0).astype(F32) + head_near[0].astype(F32) + head_near[1].astype(F32)

    shape = head_out.shape
    return layer_out.reshape(shape), head_grad.astype(BF).reshape(shape), weight_sum * grad_scale, table_grad


def solution(mesh):
    fine = Mesh(mesh.devices.reshape(XH, NY, NZ, XL, NC), ("xh", "y", "z", "xl", "c"))
    dp, mp = ("xh", "y", "z"), ("xl", "c")
    tokens = P(None, dp, mp)
    return jax.shard_map(
        on_device,
        mesh=fine,
        in_specs=(tokens, tokens, P(dp, mp), P(None, mp), P(), P(None, dp), tokens),
        out_specs=(tokens, tokens, P(dp, mp), P(None, mp)),
        check_vma=False,
    )
```
